32 devices in a mesh: head: 4 (over y, x), seq: 8 (over z, core).
Axes of the slice: x: 2, y: 2, z: 4, core: 2. Of those that a mesh axis runs over, the one named last changes fastest.
Arguments:
- seq_input: bfloat16 [8192, 8192], P('seq', 'head'), may hold values from -6 to 6
- step_size: float32 [128, 8192], P('head', 'seq'), may hold values from 0.25 to 2
- decay_rate: float32 [128], P('head'), may hold values from 0 to 0.03, as said below
- skip_gain: float32 [128], P('head'), may hold values from 0.5 to 1.5
- state_write: bfloat16 [8192, 1024], P('seq', 'head'), may hold values from -0.44921875 to 0.44921875
- state_read: bfloat16 [8192, 1024], P('seq', 'head'), may hold values from -0.44921875 to 0.44921875
- out_grad: bfloat16 [8192, 8192], P('seq', 'head'), may hold values from -1.5 to 1.5
- segment_order: int32 [8], replicated, may hold values from 0 to 7, each once
- doc_start: int32 [32], replicated, may hold values from 0 to 256, as said below
Outputs:
- mixed_out: bfloat16 [8192, 8192], P('seq', 'head')
- input_grad: bfloat16 [8192, 8192], P('seq', 'head')
- write_grad: float32 [8192, 1024], P('seq', 'head')
- read_grad: float32 [8192, 1024], P('seq', 'head')
The draws below stay inside these ranges and needn't reach their ends.
Inputs may be any that keep to these rules, and one draw needn't show every extreme that they name: Shard k along seq holds sequence segment segment_order[k]; every segment once. A document starts at position doc_start[b] of stored block b, and 256 means that none starts in it; some block starts one at its first token and some block has none. `decay_rate`: positive.
All inputs are finite; a program needn't handle non-finite values.
Results may differ from the reference program's by a relative error of at most 0.0095.
Values may be sent and summed in bfloat16 or wider, within the bound.
A program may use at most 128 MiB of HBM per device.

```python
import math
import jax
import jax.numpy as jnp
from jax import lax

HEADS = 128
HEAD_DIM = 64
STATE = 128
GROUPS = 8
BLOCK = 256
BLK_DEV = 4
NBLK = 32
TOKENS = 8192
N_SEQ = 8


def draw_decay_rate(key, part):
    keys = jax.random.split(key, 2)
    spread = jax.random.uniform(keys[0], (HEADS,), jnp.float32)
    pick = jax.random.uniform(keys[1], (HEADS,), jnp.float32)
    share = 0.5
    slow_rate = jnp.exp(math.log(0.1 / TOKENS) + spread * math.log(20.0))
    fast_rate = jnp.exp(math.log(0.003) + spread * math.log(10.0))
    return jnp.where(pick < share, slow_rate, fast_rate).astype(jnp.float32)


def draw_doc_start(key, part):
    keys = jax.random.split(key, 4)
    places = jax.random.randint(keys[0], (NBLK,), 0, BLOCK)
    chance = jax.random.randint(keys[1], (NBLK,), 0, 16)
    starts = jnp.where(chance == 0, places, BLOCK)
    first_pick = jax.random.randint(keys[2], (), 0, NBLK)
    second_pick = (first_pick + 1 + jax.random.randint(keys[3], (), 0, NBLK - 1)) % NBLK
    starts = starts.at[first_pick].set(BLOCK).at[second_pick].set(0)
    return starts.astype(jnp.int32)


def level_of(key, shape, cuts, low, largest):
    factor_of = 1.0
    for position, blocks in cuts:
        steps = jax.random.uniform(jax.random.fold_in(jax.random.fold_in(key, 6), position), (blocks,), jnp.float32, low / len(cuts), largest / len(cuts))
        factor_of = factor_of * jnp.repeat(jnp.exp(steps), shape[position] // blocks).reshape((-1,) + (1,) * (len(shape) - 1 - position))
    return factor_of


def scatter_about(rng, extent, scale, reach, cuts=(), kind=jnp.bfloat16):
    values = scale * jax.random.normal(rng, extent, jnp.float32)
    if cuts:
        values = values * level_of(rng, extent, cuts, -0.22, 0.18)
    return jnp.clip(values, -reach, reach).astype(kind)


def setup_inputs(seed: int = 0) -> dict:
    splits = jax.random.split(jax.random.key(seed), 10)
    seq_input = scatter_about(splits[0], (TOKENS, HEADS * HEAD_DIM), 1.0, 6.0, ((0, 8), (1, 4)))
    step_size = jnp.clip(jnp.exp(math.log(2.0) - 2.0794415 * jax.random.uniform(splits[1], (HEADS, TOKENS), jnp.float32) ** level_of(splits[1], (HEADS, TOKENS), ((0, 4), (1, 8)), -0.2, 0.2)), 0.25, 2.0)
    decay_rate = draw_decay_rate(jax.random.fold_in(splits[9], 71), 0)
    skip_gain = jnp.clip(1.0 + 0.1 * jax.random.normal(splits[3], (HEADS,), jnp.float32), 0.5, 1.5)
    state_write = scatter_about(splits[4], (TOKENS, GROUPS * STATE), 0.074, 0.44921875, ((0, 8), (1, 4)))
    state_read = scatter_about(splits[5], (TOKENS, GROUPS * STATE), 0.074, 0.44921875, ((0, 8), (1, 4)))
    out_grad = scatter_about(splits[6], (TOKENS, HEADS * HEAD_DIM), 0.25, 1.5, ((0, 8), (1, 4)))
    segment_order = jax.random.permutation(splits[7], N_SEQ).astype(jnp.int32)
    doc_start = draw_doc_start(jax.random.fold_in(splits[9], 71), 0)
    return dict(seq_input=seq_input, step_size=step_size, decay_rate=decay_rate, skip_gain=skip_gain, state_write=state_write, state_read=state_read, out_grad=out_grad, segment_order=segment_order, doc_start=doc_start)


HIGHEST_PRECISION = lax.Precision.HIGHEST


def lift(array):
    return array.astype(jnp.float32)


def decay_terms(step_block, decay_rate, doc_pos):
    length = step_block.shape[-1]
    positions = jnp.arange(length, dtype=jnp.int32)
    cum_decay = jnp.cumsum(-decay_rate[:, :, None] * step_block, axis=-1)
    after_row = positions[:, None] >= doc_pos
    before_col = positions[None, :] < doc_pos
    same_doc = (positions[:, None] >= positions[None, :]) & jnp.logical_not(after_row & before_col)
    log_gap = cum_decay[:, :, :, None] - cum_decay[:, :, None, :]
    decay_matrix = jnp.where(same_doc, jnp.exp(jnp.where(same_doc, log_gap, 0.0)), 0.0)
    read_weight = jnp.exp(cum_decay) * (positions < doc_pos).astype(jnp.float32)
    write_weight = jnp.exp(cum_decay[:, :, -1:] - cum_decay) * (positions >= doc_pos).astype(jnp.float32)
    return cum_decay, decay_matrix, read_weight, write_weight


def summaries(seq_block, step_block, write_block, read_block, grad_block, doc_pos, decay_rate):
    cum_decay, decay_matrix, read_weight, write_weight = decay_terms(step_block, decay_rate, doc_pos)
    step_cols = jnp.transpose(step_block, (2, 0, 1))[..., None]
    write_cols = jnp.transpose(write_weight, (2, 0, 1))[..., None]
    read_cols = jnp.transpose(read_weight, (2, 0, 1))[..., None]
    end_inputs = (write_cols * step_cols * lift(seq_block)).astype(jnp.bfloat16)
    weighted_grad = (read_cols * lift(grad_block)).astype(jnp.bfloat16)
    end_state = jnp.einsum("tghp,tgn->ghpn", lift(end_inputs), lift(write_block))
    read_state = jnp.einsum("tghp,tgn->ghpn", lift(weighted_grad), lift(read_block))
    return cum_decay, decay_matrix, read_cols, write_cols, step_cols, end_inputs, weighted_grad, end_state, read_state


def finish_block(seq_block, step_block, write_block, read_block, grad_block, doc_pos, decay_rate, skip_gain, state_now, grad_now):
    parts = summaries(seq_block, step_block, write_block, read_block, grad_block, doc_pos, decay_rate)
    decay_matrix, read_cols, write_cols, step_cols = parts[1], parts[2], parts[3], parts[4]
    end_inputs, weighted_grad = parts[5], parts[6]
    inputs = (step_cols * lift(seq_block)).astype(jnp.bfloat16)
    scores = jnp.einsum("tgn,sgn->gts", lift(read_block), lift(write_block))
    mixer = (scores[:, None] * decay_matrix).astype(jnp.bfloat16)
    intra_out = jnp.einsum("ghts,sghp->tghp", lift(mixer), lift(inputs))
    carried = jnp.einsum("tgn,ghpn->tghp", lift(read_block), state_now, precision=HIGHEST_PRECISION)
    skips = skip_gain[None, :, :, None]
    mixed = (intra_out + read_cols * carried + skips * lift(seq_block)).astype(jnp.bfloat16)
    mixer_grad = jnp.einsum("tghp,sghp->ghts", lift(grad_block), lift(inputs))
    score_grad = (mixer_grad * decay_matrix).astype(jnp.bfloat16)
    intra_grad = jnp.einsum("ghts,tghp->sghp", lift(mixer), lift(grad_block))
    back_term = jnp.einsum("tgn,ghpn->tghp", lift(write_block), grad_now, precision=HIGHEST_PRECISION)
    input_grad = (skips * lift(grad_block) + step_cols * (intra_grad + write_cols * back_term)).astype(jnp.bfloat16)
    write_grad = jnp.einsum("ghts,tgn->sgn", lift(score_grad), lift(read_block)) + jnp.einsum("tghp,ghpn->tgn", lift(end_inputs), grad_now, precision=HIGHEST_PRECISION)
    read_grad = jnp.einsum("ghts,sgn->tgn", lift(score_grad), lift(write_block)) + jnp.einsum("tghp,ghpn->tgn", lift(weighted_grad), state_now, precision=HIGHEST_PRECISION)
    return mixed, input_grad, write_grad, read_grad


def reference(seq_input, step_size, decay_rate, skip_gain, state_write, state_read, out_grad, segment_order, doc_start):
    group_heads = HEADS // GROUPS
    seq_blocks = seq_input.reshape(NBLK, BLOCK, GROUPS, group_heads, HEAD_DIM)
    grad_blocks = out_grad.reshape(NBLK, BLOCK, GROUPS, group_heads, HEAD_DIM)
    write_blocks = state_write.reshape(NBLK, BLOCK, GROUPS, STATE)
    read_blocks = state_read.reshape(NBLK, BLOCK, GROUPS, STATE)
    step_blocks = jnp.transpose(step_size.reshape(GROUPS, group_heads, NBLK, BLOCK), (2, 0, 1, 3))
    rates = decay_rate.reshape(GROUPS, group_heads)
    skips = skip_gain.reshape(GROUPS, group_heads)

    def first_pass(items):
        parts = summaries(items[0], items[1], items[2], items[3], items[4], items[5], rates)
        return parts[0][:, :, -1], parts[7], parts[8]

    block_log, end_states, read_states = lax.map(first_pass, (seq_blocks, step_blocks, write_blocks, read_blocks, grad_blocks, doc_start))
    resets = (doc_start < BLOCK).astype(jnp.float32)
    block_decay = jnp.exp(block_log) * (1.0 - resets)[:, None, None]
    seq_of_stored = (segment_order[:, None] * BLK_DEV + jnp.arange(BLK_DEV, dtype=jnp.int32)[None, :]).reshape(NBLK).astype(jnp.int32)
    stored_of_seq = jnp.zeros((NBLK,), jnp.int32).at[seq_of_stored].set(jnp.arange(NBLK, dtype=jnp.int32))
    decay_seq = block_decay[stored_of_seq]
    end_seq = end_states[stored_of_seq]
    read_seq = read_states[stored_of_seq]

    def forward(carry, item):
        return item[0][:, :, None, None] * carry + item[1], carry

    def backward(carry, item):
        return item[1] + item[0][:, :, None, None] * carry, carry

    empty = jnp.zeros((GROUPS, group_heads, HEAD_DIM, STATE), jnp.float32)
    final_state, state_in_seq = lax.scan(forward, empty, (decay_seq, end_seq))
    first_grad, grad_next_seq = lax.scan(backward, empty, (decay_seq, read_seq), reverse=True)
    state_in = state_in_seq[seq_of_stored]
    grad_next = grad_next_seq[seq_of_stored]

    def second_pass(items):
        return finish_block(items[0], items[1], items[2], items[3], items[4], items[5], rates, skips, items[6], items[7])

    mixed, input_grad, write_grad, read_grad = lax.map(second_pass, (seq_blocks, step_blocks, write_blocks, read_blocks, grad_blocks, doc_start, state_in, grad_next))
    return (mixed.reshape(TOKENS, HEADS * HEAD_DIM), input_grad.reshape(TOKENS, HEADS * HEAD_DIM), write_grad.reshape(TOKENS, GROUPS * STATE), read_grad.reshape(TOKENS, GROUPS * STATE))
```

```python
import functools

import jax
import jax.numpy as jnp
from jax import lax
from jax.experimental import pallas as pl
from jax.experimental.pallas import tpu as pltpu
from jax.sharding import PartitionSpec as P

HEADS = 128
HEAD_DIM = 64
STATE = 128
GROUPS = 8
BLOCK = 256
CHUNK = 256
EXTRA = 16
VMEM_LIMIT = 50 * 1024 * 1024

F32 = jnp.float32
BF16 = jnp.bfloat16


def partner(block, axis, bit):
    count = lax.axis_size(axis)
    route = []
    for low in range(count):
        high = low | 1 << bit
        if high != low and high < count:
            route += [(low, high), (high, low)]
    return lax.ppermute(block, axis, route)


def dot_nn(a, b):
    return lax.dot_general(a, b, (((1,), (0,)), ((), ())), preferred_element_type=F32)


def dot_nt(a, b):
    return lax.dot_general(a, b, (((1,), (1,)), ((), ())), preferred_element_type=F32)


def dot_tn(a, b):
    return lax.dot_general(a, b, (((0,), (0,)), ((), ())), preferred_element_type=F32)


def iota(shape, dim):
    return lax.broadcasted_iota(jnp.int32, shape, dim)


def head_spread(heads, first_head, width):
    row = iota((2 * heads, width), 0)
    row = jnp.where(row >= heads, row - heads, row)
    return (row == first_head + iota((2 * heads, width), 1) // HEAD_DIM).astype(F32).astype(BF16)


def token_weights(step, rate):
    heads, length = step.shape
    both = jnp.concatenate([step, step], axis=0)
    row, col = iota((length, length), 0), iota((length, length), 1)
    lower = (row >= col).astype(F32).astype(BF16)
    eye = (row == col).astype(F32).astype(BF16)
    high = both.astype(BF16)
    rest = both - high.astype(F32)
    mid = rest.astype(BF16)
    low = (rest - mid.astype(F32)).astype(BF16)
    cum = -rate * (dot_nt(lower, high) + dot_nt(lower, mid) + dot_nt(lower, low))
    cols = dot_nt(eye, high) + dot_nt(eye, mid) + dot_nt(eye, low)
    left = iota((length, 2 * heads), 1) < heads

    def halves(value):
        top = value.astype(BF16).astype(F32)
        return jnp.where(left, top, value - top).astype(BF16)

    return halves(jnp.exp(cum)), halves(cols * jnp.exp(-cum))


def summary_kernel(
    heads,
    blocks,
    doc_ref,
    x_ref,
    g_ref,
    step_ref,
    rate_ref,
    b_ref,
    c_ref,
    msg_ref,
    pre_ref,
    suf_ref,
    scale_ref,
    e_ref,
    f_ref,
):
    chunk = pl.program_id(0)

    @pl.when(chunk == 0)
    def _():
        for k in range(blocks):
            rows = pl.ds(k * BLOCK, BLOCK)
            e_ref[rows, :], f_ref[rows, :] = token_weights(step_ref[:, rows], rate_ref[...])

    spread = head_spread(heads, chunk * (CHUNK // HEAD_DIM), CHUNK)
    position = iota((BLOCK, STATE), 0)
    ends, reads, decays = [], [], []
    for k in range(blocks):
        rows = pl.ds(k * BLOCK, BLOCK)
        doc = doc_ref[k]
        e_wide = dot_nn(e_ref[rows, :], spread)
        f_wide = dot_nn(f_ref[rows, :], spread)
        grad_in = (e_wide * g_ref[rows, :].astype(F32)).astype(BF16)
        data_in = (f_wide * x_ref[rows, :].astype(F32)).astype(BF16)
        write = jnp.where(position >= doc, b_ref[rows, :].astype(F32), 0.0).astype(BF16)
        read = jnp.where(position < doc, c_ref[rows, :].astype(F32), 0.0).astype(BF16)
        last = e_wide[BLOCK - 1 : BLOCK, :]
        ends.append(last * dot_tn(write, data_in))
        reads.append(dot_tn(read, grad_in))
        decays.append(jnp.where(doc == BLOCK, last, 0.0))
    state = jnp.zeros((STATE, CHUNK), F32)
    lead = jnp.ones((1, CHUNK), F32)
    for k in range(blocks):
        pre_ref[k] = state.astype(BF16)
        scale_ref[k : k + 1, :] = lead
        state = decays[k] * state + ends[k]
        lead = lead * decays[k]
    grad = jnp.zeros((STATE, CHUNK), F32)
    tail = jnp.ones((1, CHUNK), F32)
    for k in reversed(range(blocks)):
        suf_ref[k] = grad.astype(BF16)
        scale_ref[blocks + k : blocks + k + 1, :] = tail
        grad = reads[k] + decays[k] * grad
        tail = tail * decays[k]
    msg_ref[0, :STATE, :] = state.astype(BF16)
    msg_ref[0, STATE : 2 * STATE, :] = grad.astype(BF16)
    top = jnp.broadcast_to(lead, (EXTRA, CHUNK)).astype(BF16).astype(F32)
    rest = jnp.broadcast_to(lead, (EXTRA, CHUNK)) - top
    msg_ref[0, 2 * STATE :, :] = jnp.where(iota((EXTRA, CHUNK), 0) == 0, top, rest).astype(BF16)


def chain_kernel(count, order_ref, got_ref, out_ref):
    width = got_ref.shape[-1]

    def decay_of(shard):
        pair = got_ref[shard, 2 * STATE :, :].astype(F32)
        return pair[0:1, :] + pair[1:2, :]

    def forward(place, state):
        shard = order_ref[place]
        out_ref[shard, :STATE, :] = state.astype(BF16)
        return decay_of(shard) * state + got_ref[shard, :STATE, :].astype(F32)

    def backward(step, grad):
        shard = order_ref[count - 1 - step]
        out_ref[shard, STATE:, :] = grad.astype(BF16)
        return decay_of(shard) * grad + got_ref[shard, STATE : 2 * STATE, :].astype(F32)

    empty = jnp.zeros((STATE, width), F32)
    lax.fori_loop(0, count, forward, empty)
    lax.fori_loop(0, count, backward, empty)


def finish_kernel(
    heads,
    blocks,
    span,
    doc_ref,
    x_ref,
    g_ref,
    b_ref,
    c_ref,
    e_ref,
    f_ref,
    pre_ref,
    suf_ref,
    scale_ref,
    dev_ref,
    skip_ref,
    y_ref,
    dx_ref,
    dw_ref,
    dr_ref,
):
    group, k = pl.program_id(0), pl.program_id(1)
    doc = doc_ref[k]
    width = span * HEAD_DIM
    spread = head_spread(heads, group * span, width)
    e_wide = dot_nn(e_ref[...], spread)
    f_wide = dot_nn(f_ref[...], spread)
    x = x_ref[...].astype(F32)
    g = g_ref[...].astype(F32)
    grad_in = (e_wide * g).astype(BF16)
    data_in = (f_wide * x).astype(BF16)
    position = iota((BLOCK, STATE), 0)
    b, c = b_ref[...], c_ref[...]
    write_on, read_on = position >= doc, position < doc
    write = jnp.where(write_on, b.astype(F32), 0.0).astype(BF16)
    read = jnp.where(read_on, c.astype(F32), 0.0).astype(BF16)
    state_dev = jnp.concatenate([dev_ref[j, :STATE, :] for j in range(dev_ref.shape[0])], axis=1)
    grad_dev = jnp.concatenate([dev_ref[j, STATE:, :] for j in range(dev_ref.shape[0])], axis=1)
    scales = scale_ref[...]
    which = iota(scales.shape, 0)
    lead = jnp.sum(jnp.where(which == k, scales, 0.0), axis=0, keepdims=True)
    tail = jnp.sum(jnp.where(which == blocks + k, scales, 0.0), axis=0, keepdims=True)
    last = e_wide[BLOCK - 1 : BLOCK, :]
    state = (pre_ref[0].astype(F32) + lead * state_dev.astype(F32)).astype(BF16)
    grad = (last * (suf_ref[0].astype(F32) + tail * grad_dev.astype(F32))).astype(BF16)
    row, col = iota((BLOCK, BLOCK), 0), iota((BLOCK, BLOCK), 1)
    keep = (row >= col) & ((row < doc) | (col >= doc))
    keep_t = (col >= row) & ((col < doc) | (row >= doc))
    score = jnp.where(keep, dot_nt(c, b), 0.0).astype(BF16)
    score_t = jnp.where(keep_t, dot_nt(b, c), 0.0).astype(BF16)
    skip = skip_ref[...]
    y_ref[...] = (e_wide * (dot_nn(score, data_in) + dot_nn(read, state)) + skip * x).astype(BF16)
    dx_ref[...] = (f_wide * (dot_nn(score_t, grad_in) + dot_nn(write, grad)) + skip * g).astype(
        BF16
    )
    score_grad = jnp.where(keep, dot_nt(grad_in, data_in), 0.0).astype(BF16)
    dw_ref[...] = dot_tn(score_grad, c) + jnp.where(write_on, dot_nt(data_in, grad), 0.0)
    dr_ref[...] = dot_nn(score_grad, b) + jnp.where(read_on, dot_nt(grad_in, state), 0.0)


def on_device(
    seq_input,
    step_size,
    decay_rate,
    skip_gain,
    state_write,
    state_read,
    out_grad,
    segment_order,
    doc_start,
):
    heads = decay_rate.shape[0]
    group_heads = HEADS // GROUPS
    span = min(heads, group_heads)
    groups = heads // span
    group_devices = max(1, group_heads // heads)
    levels = group_devices.bit_length() - 1
    tokens = seq_input.shape[0]
    blocks = tokens // BLOCK
    channels = heads * HEAD_DIM
    chunks = channels // CHUNK
    group_chunks = chunks // groups
    seq_count = lax.axis_size("seq")
    head_rank = lax.axis_index("head")
    seq_rank = lax.axis_index("seq")
    own_write, own_read = (state_write, state_read)
    for level in range(levels):
        other_write, other_read = partner((own_write, own_read), "head", level)
        upper_half = head_rank >> level & 1 == 1
        own_write = jnp.where(
            upper_half,
            jnp.concatenate([other_write, own_write], 1),
            jnp.concatenate([own_write, other_write], 1),
        )
        own_read = jnp.where(
            upper_half,
            jnp.concatenate([other_read, own_read], 1),
            jnp.concatenate([own_read, other_read], 1),
        )
    doc_here = lax.dynamic_slice_in_dim(doc_start, seq_rank * blocks, blocks)
    rate_row = jnp.concatenate([decay_rate, decay_rate]).reshape(1, 2 * heads)
    skip_row = jnp.repeat(skip_gain, HEAD_DIM).reshape(1, channels)
    smem = pl.BlockSpec(memory_space=pltpu.SMEM)
    params = pltpu.CompilerParams(vmem_limit_bytes=VMEM_LIMIT)
    rows = 2 * STATE + EXTRA

    message, pre, suf, scales, e_cols, f_cols = pl.pallas_call(
        functools.partial(summary_kernel, heads, blocks),
        grid=(chunks,),
        out_shape=(
            jax.ShapeDtypeStruct((chunks, rows, CHUNK), BF16),
            jax.ShapeDtypeStruct((blocks, STATE, channels), BF16),
            jax.ShapeDtypeStruct((blocks, STATE, channels), BF16),
            jax.ShapeDtypeStruct((2 * blocks, channels), F32),
            jax.ShapeDtypeStruct((tokens, 2 * heads), BF16),
            jax.ShapeDtypeStruct((tokens, 2 * heads), BF16),
        ),
        in_specs=[
            smem,
            pl.BlockSpec((tokens, CHUNK), lambda i: (0, i)),
            pl.BlockSpec((tokens, CHUNK), lambda i: (0, i)),
            pl.BlockSpec((heads, tokens), lambda i: (0, 0)),
            pl.BlockSpec((1, 2 * heads), lambda i: (0, 0)),
            pl.BlockSpec((tokens, STATE), lambda i: (0, i // group_chunks)),
            pl.BlockSpec((tokens, STATE), lambda i: (0, i // group_chunks)),
        ],
        out_specs=(
            pl.BlockSpec((1, rows, CHUNK), lambda i: (i, 0, 0)),
            pl.BlockSpec((blocks, STATE, CHUNK), lambda i: (0, 0, i)),
            pl.BlockSpec((blocks, STATE, CHUNK), lambda i: (0, 0, i)),
            pl.BlockSpec((2 * blocks, CHUNK), lambda i: (0, i)),
            pl.BlockSpec((tokens, 2 * heads), lambda i: (0, 0)),
            pl.BlockSpec((tokens, 2 * heads), lambda i: (0, 0)),
        ),
        compiler_params=params,
        name="summary",
    )(doc_here, seq_input, out_grad, step_size, rate_row, own_write, own_read)

    width = channels // seq_count
    direct = chunks == seq_count
    if not direct:
        message = jnp.transpose(message, (1, 0, 2)).reshape(rows, seq_count, width)
        message = jnp.transpose(message, (1, 0, 2))
    got = lax.all_to_all(message, "seq", split_axis=0, concat_axis=0, tiled=True)
    order = jnp.zeros((seq_count,), jnp.int32).at[segment_order].set(
        jnp.arange(seq_count, dtype=jnp.int32)
    )
    answer = pl.pallas_call(
        functools.partial(chain_kernel, seq_count),
        out_shape=jax.ShapeDtypeStruct((seq_count, 2 * STATE, width), BF16),
        in_specs=[smem, pl.BlockSpec(memory_space=pltpu.VMEM)],
        out_specs=pl.BlockSpec(memory_space=pltpu.VMEM),
        compiler_params=params,
        name="chain",
    )(order, got)
    device = lax.all_to_all(answer, "seq", split_axis=0, concat_axis=0, tiled=True)
    if not direct:
        device = jnp.transpose(device, (1, 0, 2)).reshape(2 * STATE, chunks, CHUNK)
        device = jnp.transpose(device, (1, 0, 2))

    lanes = span * HEAD_DIM
    mixed, input_grad, write_sum, read_sum = pl.pallas_call(
        functools.partial(finish_kernel, heads, blocks, span),
        grid=(groups, blocks),
        out_shape=(
            jax.ShapeDtypeStruct((tokens, channels), BF16),
            jax.ShapeDtypeStruct((tokens, channels), BF16),
            jax.ShapeDtypeStruct((tokens, groups * STATE), F32),
            jax.ShapeDtypeStruct((tokens, groups * STATE), F32),
        ),
        in_specs=[
            smem,
            pl.BlockSpec((BLOCK, lanes), lambda g, k: (k, g)),
            pl.BlockSpec((BLOCK, lanes), lambda g, k: (k, g)),
            pl.BlockSpec((BLOCK, STATE), lambda g, k: (k, g)),
            pl.BlockSpec((BLOCK, STATE), lambda g, k: (k, g)),
            pl.BlockSpec((BLOCK, 2 * heads), lambda g, k: (k, 0)),
            pl.BlockSpec((BLOCK, 2 * heads), lambda g, k: (k, 0)),
            pl.BlockSpec((1, STATE, lanes), lambda g, k: (k, 0, g)),
            pl.BlockSpec((1, STATE, lanes), lambda g, k: (k, 0, g)),
            pl.BlockSpec((2 * blocks, lanes), lambda g, k: (0, g)),
            pl.BlockSpec((group_chunks, 2 * STATE, CHUNK), lambda g, k: (g, 0, 0)),
            pl.BlockSpec((1, lanes), lambda g, k: (0, g)),
        ],
        out_specs=(
            pl.BlockSpec((BLOCK, lanes), lambda g, k: (k, g)),
            pl.BlockSpec((BLOCK, lanes), lambda g, k: (k, g)),
            pl.BlockSpec((BLOCK, STATE), lambda g, k: (k, g)),
            pl.BlockSpec((BLOCK, STATE), lambda g, k: (k, g)),
        ),
        compiler_params=params,
        name="finish",
    )(
        doc_here,
        seq_input,
        out_grad,
        own_write,
        own_read,
        e_cols,
        f_cols,
        pre,
        suf,
        scales,
        device,
        skip_row,
    )

    for level in range(levels):
        other_write_sum, other_read_sum = partner(
            (write_sum.astype(BF16), read_sum.astype(BF16)), "head", level
        )
        write_sum = write_sum + other_write_sum.astype(F32)
        read_sum = read_sum + other_read_sum.astype(F32)
    own_width = groups * STATE // group_devices
    if group_devices > 1:
        own_first = head_rank % group_devices * own_width
        write_sum = lax.dynamic_slice_in_dim(write_sum, own_first, own_width, 1)
        read_sum = lax.dynamic_slice_in_dim(read_sum, own_first, own_width, 1)
    return mixed, input_grad, write_sum, read_sum


def solution(mesh):
    placed = (
        P("seq", "head"),
        P("head", "seq"),
        P("head"),
        P("head"),
        P("seq", "head"),
        P("seq", "head"),
        P("seq", "head"),
        P(),
        P(),
    )
    return jax.shard_map(
        on_device,
        mesh=mesh,
        in_specs=placed,
        out_specs=(P("seq", "head"), P("seq", "head"), P("seq", "head"), P("seq", "head")),
        check_vma=False,
    )
```

```python
import functools

import jax
import jax.numpy as jnp
from jax import lax
from jax.experimental import pallas as pl
from jax.experimental.pallas import tpu as pltpu
from jax.sharding import PartitionSpec as P

HEADS = 128
HEAD_DIM = 64
STATE = 128
GROUPS = 8
BLOCK = 256
CHUNK = 256
EXTRA = 16
VMEM_LIMIT = 60 * 1024 * 1024

F32 = jnp.float32
BF16 = jnp.bfloat16


def partner(block, axis, bit):
    count = lax.axis_size(axis)
    route = []
    for low in range(count):
        high = low | 1 << bit
        if high != low and high < count:
            route += [(low, high), (high, low)]
    return lax.ppermute(block, axis, route)


def dot_nn(a, b):
    return lax.dot_general(a, b, (((1,), (0,)), ((), ())), preferred_element_type=F32)


def dot_nt(a, b):
    return lax.dot_general(a, b, (((1,), (1,)), ((), ())), preferred_element_type=F32)


def dot_tn(a, b):
    return lax.dot_general(a, b, (((0,), (0,)), ((), ())), preferred_element_type=F32)


def iota(shape, dim):
    return lax.broadcasted_iota(jnp.int32, shape, dim)


def head_spread(heads, first_head, width):
    row = iota((2 * heads, width), 0)
    row = jnp.where(row >= heads, row - heads, row)
    return (row == first_head + iota((2 * heads, width), 1) // HEAD_DIM).astype(F32).astype(BF16)


def token_weights(step, rate):
    heads, length = step.shape
    both = jnp.concatenate([step, step], axis=0)
    row, col = iota((length, length), 0), iota((length, length), 1)
    lower = (row >= col).astype(F32).astype(BF16)
    eye = (row == col).astype(F32).astype(BF16)
    high = both.astype(BF16)
    rest = both - high.astype(F32)
    mid = rest.astype(BF16)
    low = (rest - mid.astype(F32)).astype(BF16)
    cum = -rate * (dot_nt(lower, high) + dot_nt(lower, mid) + dot_nt(lower, low))
    cols = dot_nt(eye, high) + dot_nt(eye, mid) + dot_nt(eye, low)
    left = iota((length, 2 * heads), 1) < heads

    def halves(value):
        top = value.astype(BF16).astype(F32)
        return jnp.where(left, top, value - top).astype(BF16)

    return halves(jnp.exp(cum)), halves(cols * jnp.exp(-cum))


def owner_at(step, count):
    return lax.rem(step, 2) * (count // 2) + step // 2


def summary_kernel(
    heads,
    blocks,
    chunk,
    first,
    doc_ref,
    x_ref,
    g_ref,
    step_ref,
    rate_ref,
    b_ref,
    c_ref,
    msg_ref,
    slot,
    pre_ref,
    suf_ref,
    scale_ref,
    e_ref,
    f_ref,
):
    @pl.when(first)
    def _():
        for k in range(blocks):
            rows = pl.ds(k * BLOCK, BLOCK)
            e_ref[rows, :], f_ref[rows, :] = token_weights(step_ref[:, rows], rate_ref[...])

    spread = head_spread(heads, chunk * (CHUNK // HEAD_DIM), CHUNK)
    position = iota((BLOCK, STATE), 0)
    ends, reads, decays = [], [], []
    for k in range(blocks):
        rows = pl.ds(k * BLOCK, BLOCK)
        doc = doc_ref[k]
        e_wide = dot_nn(e_ref[rows, :], spread)
        f_wide = dot_nn(f_ref[rows, :], spread)
        grad_in = (e_wide * g_ref[rows, :].astype(F32)).astype(BF16)
        data_in = (f_wide * x_ref[rows, :].astype(F32)).astype(BF16)
        write = jnp.where(position >= doc, b_ref[rows, :].astype(F32), 0.0).astype(BF16)
        read = jnp.where(position < doc, c_ref[rows, :].astype(F32), 0.0).astype(BF16)
        last = e_wide[BLOCK - 1 : BLOCK, :]
        ends.append(last * dot_tn(write, data_in))
        reads.append(dot_tn(read, grad_in))
        decays.append(jnp.where(doc == BLOCK, last, 0.0))
    state = jnp.zeros((STATE, CHUNK), F32)
    lead = jnp.ones((1, CHUNK), F32)
    for k in range(blocks):
        pre_ref[k] = state.astype(BF16)
        scale_ref[k : k + 1, :] = lead
        state = decays[k] * state + ends[k]
        lead = lead * decays[k]
    grad = jnp.zeros((STATE, CHUNK), F32)
    tail = jnp.ones((1, CHUNK), F32)
    for k in reversed(range(blocks)):
        suf_ref[k] = grad.astype(BF16)
        scale_ref[blocks + k : blocks + k + 1, :] = tail
        grad = reads[k] + decays[k] * grad
        tail = tail * decays[k]
    msg_ref[slot, :STATE, :] = state.astype(BF16)
    msg_ref[slot, STATE : 2 * STATE, :] = grad.astype(BF16)
    top = jnp.broadcast_to(lead, (EXTRA, CHUNK)).astype(BF16).astype(F32)
    rest = jnp.broadcast_to(lead, (EXTRA, CHUNK)) - top
    msg_ref[slot, 2 * STATE :, :] = jnp.where(iota((EXTRA, CHUNK), 0) == 0, top, rest).astype(BF16)


def summary_call(heads, blocks, *refs):
    chunk = pl.program_id(0)
    msg_ref = refs[7]
    summary_kernel(heads, blocks, chunk, chunk == 0, *refs[:7], msg_ref, 0, *refs[8:])


def chain_kernel(count, order_ref, got_ref, out_ref):
    width = got_ref.shape[-1]

    def decay_of(shard):
        pair = got_ref[shard, 2 * STATE :, :].astype(F32)
        return pair[0:1, :] + pair[1:2, :]

    def forward(place, state):
        shard = order_ref[place]
        out_ref[shard, :STATE, :] = state.astype(BF16)
        return decay_of(shard) * state + got_ref[shard, :STATE, :].astype(F32)

    def backward(step, grad):
        shard = order_ref[count - 1 - step]
        out_ref[shard, STATE:, :] = grad.astype(BF16)
        return decay_of(shard) * grad + got_ref[shard, STATE : 2 * STATE, :].astype(F32)

    empty = jnp.zeros((STATE, width), F32)
    lax.fori_loop(0, count, forward, empty)
    lax.fori_loop(0, count, backward, empty)


def exchange_kernel(
    heads,
    blocks,
    count,
    doc_ref,
    order_ref,
    place_ref,
    x_ref,
    g_ref,
    step_ref,
    rate_ref,
    b_ref,
    c_ref,
    pre_ref,
    suf_ref,
    scale_ref,
    e_ref,
    f_ref,
    dev_ref,
    msg,
    got,
    chain,
    answer,
    back,
    send_sem,
    recv_sem,
    back_send_sem,
    back_recv_sem,
):
    step = pl.program_id(0)
    me = lax.axis_index("seq")
    barrier = pltpu.get_barrier_semaphore()

    def outward(owner, source):
        return pltpu.make_async_remote_copy(
            src_ref=msg.at[owner],
            dst_ref=got.at[source],
            send_sem=send_sem.at[owner],
            recv_sem=recv_sem.at[source],
            device_id={"seq": owner},
            device_id_type=pl.DeviceIdType.MESH,
        )

    def homeward(shard, source):
        return pltpu.make_async_remote_copy(
            src_ref=answer.at[shard],
            dst_ref=back.at[source],
            send_sem=back_send_sem.at[shard],
            recv_sem=back_recv_sem.at[source],
            device_id={"seq": shard},
            device_id_type=pl.DeviceIdType.MESH,
        )

    @pl.when(step == 0)
    def _():
        for ahead in range(1, count):
            pl.semaphore_signal(
                barrier,
                inc=1,
                device_id={"seq": lax.rem(me + ahead, count)},
                device_id_type=pl.DeviceIdType.MESH,
            )

    @pl.when(step < count)
    def _():
        owner = owner_at(step, count)
        summary_kernel(
            heads,
            blocks,
            owner,
            step == 0,
            doc_ref,
            x_ref,
            g_ref,
            step_ref,
            rate_ref,
            b_ref,
            c_ref,
            msg,
            owner,
            pre_ref,
            suf_ref,
            scale_ref,
            e_ref,
            f_ref,
        )

        @pl.when(step == 0)
        def _():
            pl.semaphore_wait(barrier, count - 1)

        @pl.when(owner != me)
        def _():
            outward(owner, me).start()

        @pl.when(owner == me)
        def _():
            got[me] = msg[owner]

    @pl.when(step == count)
    def _():
        for shard in range(count):

            @pl.when(me != shard)
            def _():
                outward(shard, shard).wait_recv()

        def decay_of(shard):
            pair = got[shard, 2 * STATE :, :].astype(F32)
            return pair[0:1, :] + pair[1:2, :]

        state = jnp.zeros((STATE, CHUNK), F32)
        for place in range(count):
            shard = order_ref[place]
            chain[place, :STATE, :] = state.astype(BF16)
            state = decay_of(shard) * state + got[shard, :STATE, :].astype(F32)
        grad = jnp.zeros((STATE, CHUNK), F32)
        for place in reversed(range(count)):
            shard = order_ref[place]
            chain[place, STATE:, :] = grad.astype(BF16)
            grad = decay_of(shard) * grad + got[shard, STATE : 2 * STATE, :].astype(F32)
        for shard in range(count):
            answer[shard] = chain[place_ref[shard]]

            @pl.when(me != shard)
            def _():
                homeward(shard, me).start()

        back[me] = answer[me]
        for shard in range(count):

            @pl.when(me != shard)
            def _():
                homeward(shard, shard).wait_recv()

        for shard in range(count):

            @pl.when(me != shard)
            def _():
                outward(shard, me).wait_send()
                homeward(shard, me).wait_send()

        dev_ref[...] = back[...]


def finish_kernel(
    heads,
    blocks,
    span,
    doc_ref,
    x_ref,
    g_ref,
    b_ref,
    c_ref,
    e_ref,
    f_ref,
    pre_ref,
    suf_ref,
    scale_ref,
    dev_ref,
    skip_ref,
    y_ref,
    dx_ref,
    dw_ref,
    dr_ref,
):
    group, k = pl.program_id(0), pl.program_id(1)
    doc = doc_ref[k]
    width = span * HEAD_DIM
    spread = head_spread(heads, group * span, width)
    e_wide = dot_nn(e_ref[...], spread)
    f_wide = dot_nn(f_ref[...], spread)
    x = x_ref[...].astype(F32)
    g = g_ref[...].astype(F32)
    grad_in = (e_wide * g).astype(BF16)
    data_in = (f_wide * x).astype(BF16)
    position = iota((BLOCK, STATE), 0)
    b, c = b_ref[...], c_ref[...]
    write_on, read_on = position >= doc, position < doc
    write = jnp.where(write_on, b.astype(F32), 0.0).astype(BF16)
    read = jnp.where(read_on, c.astype(F32), 0.0).astype(BF16)
    state_dev = jnp.concatenate([dev_ref[j, :STATE, :] for j in range(dev_ref.shape[0])], axis=1)
    grad_dev = jnp.concatenate([dev_ref[j, STATE:, :] for j in range(dev_ref.shape[0])], axis=1)
    scales = scale_ref[...]
    which = iota(scales.shape, 0)
    lead = jnp.sum(jnp.where(which == k, scales, 0.0), axis=0, keepdims=True)
    tail = jnp.sum(jnp.where(which == blocks + k, scales, 0.0), axis=0, keepdims=True)
    last = e_wide[BLOCK - 1 : BLOCK, :]
    state = (pre_ref[0].astype(F32) + lead * state_dev.astype(F32)).astype(BF16)
    grad = (last * (suf_ref[0].astype(F32) + tail * grad_dev.astype(F32))).astype(BF16)
    row, col = iota((BLOCK, BLOCK), 0), iota((BLOCK, BLOCK), 1)
    keep = (row >= col) & ((row < doc) | (col >= doc))
    keep_t = (col >= row) & ((col < doc) | (row >= doc))
    score = jnp.where(keep, dot_nt(c, b), 0.0).astype(BF16)
    score_t = jnp.where(keep_t, dot_nt(b, c), 0.0).astype(BF16)
    skip = skip_ref[...]
    y_ref[...] = (e_wide * (dot_nn(score, data_in) + dot_nn(read, state)) + skip * x).astype(BF16)
    dx_ref[...] = (f_wide * (dot_nn(score_t, grad_in) + dot_nn(write, grad)) + skip * g).astype(
        BF16
    )
    score_grad = jnp.where(keep, dot_nt(grad_in, data_in), 0.0).astype(BF16)
    dw_ref[...] = dot_tn(score_grad, c) + jnp.where(write_on, dot_nt(data_in, grad), 0.0)
    dr_ref[...] = dot_nn(score_grad, b) + jnp.where(read_on, dot_nt(grad_in, state), 0.0)


def on_device(
    seq_input,
    step_size,
    decay_rate,
    skip_gain,
    state_write,
    state_read,
    out_grad,
    segment_order,
    doc_start,
):
    heads = decay_rate.shape[0]
    group_heads = HEADS // GROUPS
    span = min(heads, group_heads)
    groups = heads // span
    group_devices = max(1, group_heads // heads)
    levels = group_devices.bit_length() - 1
    tokens = seq_input.shape[0]
    blocks = tokens // BLOCK
    channels = heads * HEAD_DIM
    chunks = channels // CHUNK
    group_chunks = chunks // groups
    seq_count = lax.axis_size("seq")
    head_rank = lax.axis_index("head")
    seq_rank = lax.axis_index("seq")
    own_write, own_read = (state_write, state_read)
    for level in range(levels):
        other_write, other_read = partner((own_write, own_read), "head", level)
        upper_half = head_rank >> level & 1 == 1
        own_write = jnp.where(
            upper_half,
            jnp.concatenate([other_write, own_write], 1),
            jnp.concatenate([own_write, other_write], 1),
        )
        own_read = jnp.where(
            upper_half,
            jnp.concatenate([other_read, own_read], 1),
            jnp.concatenate([own_read, other_read], 1),
        )
    doc_here = lax.dynamic_slice_in_dim(doc_start, seq_rank * blocks, blocks)
    rate_row = jnp.concatenate([decay_rate, decay_rate]).reshape(1, 2 * heads)
    skip_row = jnp.repeat(skip_gain, HEAD_DIM).reshape(1, channels)
    smem = pl.BlockSpec(memory_space=pltpu.SMEM)
    params = pltpu.CompilerParams(vmem_limit_bytes=VMEM_LIMIT)
    rows = 2 * STATE + EXTRA

    order = jnp.zeros((seq_count,), jnp.int32).at[segment_order].set(
        jnp.arange(seq_count, dtype=jnp.int32)
    )
    if chunks == seq_count:

        def served(i):
            return owner_at(jnp.minimum(i, chunks - 1), chunks)

        pre, suf, scales, e_cols, f_cols, device = pl.pallas_call(
            functools.partial(exchange_kernel, heads, blocks, seq_count),
            grid=(chunks + 1,),
            out_shape=(
                jax.ShapeDtypeStruct((blocks, STATE, channels), BF16),
                jax.ShapeDtypeStruct((blocks, STATE, channels), BF16),
                jax.ShapeDtypeStruct((2 * blocks, channels), F32),
                jax.ShapeDtypeStruct((tokens, 2 * heads), BF16),
                jax.ShapeDtypeStruct((tokens, 2 * heads), BF16),
                jax.ShapeDtypeStruct((chunks, 2 * STATE, CHUNK), BF16),
            ),
            in_specs=[
                smem,
                smem,
                smem,
                pl.BlockSpec((tokens, CHUNK), lambda i: (0, served(i))),
                pl.BlockSpec((tokens, CHUNK), lambda i: (0, served(i))),
                pl.BlockSpec((heads, tokens), lambda i: (0, 0)),
                pl.BlockSpec((1, 2 * heads), lambda i: (0, 0)),
                pl.BlockSpec((tokens, STATE), lambda i: (0, served(i) // group_chunks)),
                pl.BlockSpec((tokens, STATE), lambda i: (0, served(i) // group_chunks)),
            ],
            out_specs=(
                pl.BlockSpec((blocks, STATE, CHUNK), lambda i: (0, 0, served(i))),
                pl.BlockSpec((blocks, STATE, CHUNK), lambda i: (0, 0, served(i))),
                pl.BlockSpec((2 * blocks, CHUNK), lambda i: (0, served(i))),
                pl.BlockSpec((tokens, 2 * heads), lambda i: (0, 0)),
                pl.BlockSpec((tokens, 2 * heads), lambda i: (0, 0)),
                pl.BlockSpec((chunks, 2 * STATE, CHUNK), lambda i: (0, 0, 0)),
            ),
            scratch_shapes=[
                pltpu.VMEM((chunks, rows, CHUNK), BF16),
                pltpu.VMEM((chunks, rows, CHUNK), BF16),
                pltpu.VMEM((chunks, 2 * STATE, CHUNK), BF16),
                pltpu.VMEM((chunks, 2 * STATE, CHUNK), BF16),
                pltpu.VMEM((chunks, 2 * STATE, CHUNK), BF16),
                pltpu.SemaphoreType.DMA((chunks,)),
                pltpu.SemaphoreType.DMA((chunks,)),
                pltpu.SemaphoreType.DMA((chunks,)),
                pltpu.SemaphoreType.DMA((chunks,)),
            ],
            compiler_params=pltpu.CompilerParams(
                vmem_limit_bytes=VMEM_LIMIT, collective_id=0, has_side_effects=True
            ),
            name="exchange",
        )(
            doc_here,
            order,
            segment_order,
            seq_input,
            out_grad,
            step_size,
            rate_row,
            own_write,
            own_read,
        )
    else:
        message, pre, suf, scales, e_cols, f_cols = pl.pallas_call(
            functools.partial(summary_call, heads, blocks),
            grid=(chunks,),
            out_shape=(
                jax.ShapeDtypeStruct((chunks, rows, CHUNK), BF16),
                jax.ShapeDtypeStruct((blocks, STATE, channels), BF16),
                jax.ShapeDtypeStruct((blocks, STATE, channels), BF16),
                jax.ShapeDtypeStruct((2 * blocks, channels), F32),
                jax.ShapeDtypeStruct((tokens, 2 * heads), BF16),
                jax.ShapeDtypeStruct((tokens, 2 * heads), BF16),
            ),
            in_specs=[
                smem,
                pl.BlockSpec((tokens, CHUNK), lambda i: (0, i)),
                pl.BlockSpec((tokens, CHUNK), lambda i: (0, i)),
                pl.BlockSpec((heads, tokens), lambda i: (0, 0)),
                pl.BlockSpec((1, 2 * heads), lambda i: (0, 0)),
                pl.BlockSpec((tokens, STATE), lambda i: (0, i // group_chunks)),
                pl.BlockSpec((tokens, STATE), lambda i: (0, i // group_chunks)),
            ],
            out_specs=(
                pl.BlockSpec((1, rows, CHUNK), lambda i: (i, 0, 0)),
                pl.BlockSpec((blocks, STATE, CHUNK), lambda i: (0, 0, i)),
                pl.BlockSpec((blocks, STATE, CHUNK), lambda i: (0, 0, i)),
                pl.BlockSpec((2 * blocks, CHUNK), lambda i: (0, i)),
                pl.BlockSpec((tokens, 2 * heads), lambda i: (0, 0)),
                pl.BlockSpec((tokens, 2 * heads), lambda i: (0, 0)),
            ),
            compiler_params=params,
            name="summary",
        )(doc_here, seq_input, out_grad, step_size, rate_row, own_write, own_read)

        width = channels // seq_count
        message = jnp.transpose(message, (1, 0, 2)).reshape(rows, seq_count, width)
        message = jnp.transpose(message, (1, 0, 2))
        got = lax.all_to_all(message, "seq", split_axis=0, concat_axis=0, tiled=True)
        answer = pl.pallas_call(
            functools.partial(chain_kernel, seq_count),
            out_shape=jax.ShapeDtypeStruct((seq_count, 2 * STATE, width), BF16),
            in_specs=[smem, pl.BlockSpec(memory_space=pltpu.VMEM)],
            out_specs=pl.BlockSpec(memory_space=pltpu.VMEM),
            compiler_params=params,
            name="chain",
        )(order, got)
        device = lax.all_to_all(answer, "seq", split_axis=0, concat_axis=0, tiled=True)
        device = jnp.transpose(device, (1, 0, 2)).reshape(2 * STATE, chunks, CHUNK)
        device = jnp.transpose(device, (1, 0, 2))

    lanes = span * HEAD_DIM
    mixed, input_grad, write_sum, read_sum = pl.pallas_call(
        functools.partial(finish_kernel, heads, blocks, span),
        grid=(groups, blocks),
        out_shape=(
            jax.ShapeDtypeStruct((tokens, channels), BF16),
            jax.ShapeDtypeStruct((tokens, channels), BF16),
            jax.ShapeDtypeStruct((tokens, groups * STATE), F32),
            jax.ShapeDtypeStruct((tokens, groups * STATE), F32),
        ),
        in_specs=[
            smem,
            pl.BlockSpec((BLOCK, lanes), lambda g, k: (k, g)),
            pl.BlockSpec((BLOCK, lanes), lambda g, k: (k, g)),
            pl.BlockSpec((BLOCK, STATE), lambda g, k: (k, g)),
            pl.BlockSpec((BLOCK, STATE), lambda g, k: (k, g)),
            pl.BlockSpec((BLOCK, 2 * heads), lambda g, k: (k, 0)),
            pl.BlockSpec((BLOCK, 2 * heads), lambda g, k: (k, 0)),
            pl.BlockSpec((1, STATE, lanes), lambda g, k: (k, 0, g)),
            pl.BlockSpec((1, STATE, lanes), lambda g, k: (k, 0, g)),
            pl.BlockSpec((2 * blocks, lanes), lambda g, k: (0, g)),
            pl.BlockSpec((group_chunks, 2 * STATE, CHUNK), lambda g, k: (g, 0, 0)),
            pl.BlockSpec((1, lanes), lambda g, k: (0, g)),
        ],
        out_specs=(
            pl.BlockSpec((BLOCK, lanes), lambda g, k: (k, g)),
            pl.BlockSpec((BLOCK, lanes), lambda g, k: (k, g)),
            pl.BlockSpec((BLOCK, STATE), lambda g, k: (k, g)),
            pl.BlockSpec((BLOCK, STATE), lambda g, k: (k, g)),
        ),
        compiler_params=params,
        name="finish",
    )(
        doc_here,
        seq_input,
        out_grad,
        own_write,
        own_read,
        e_cols,
        f_cols,
        pre,
        suf,
        scales,
        device,
        skip_row,
    )

    for level in range(levels):
        other_write_sum, other_read_sum = partner(
            (write_sum.astype(BF16), read_sum.astype(BF16)), "head", level
        )
        write_sum = write_sum + other_write_sum.astype(F32)
        read_sum = read_sum + other_read_sum.astype(F32)
    own_width = groups * STATE // group_devices
    if group_devices > 1:
        own_first = head_rank % group_devices * own_width
        write_sum = lax.dynamic_slice_in_dim(write_sum, own_first, own_width, 1)
        read_sum = lax.dynamic_slice_in_dim(read_sum, own_first, own_width, 1)
    return mixed, input_grad, write_sum, read_sum


def solution(mesh):
    placed = (
        P("seq", "head"),
        P("head", "seq"),
        P("head"),
        P("head"),
        P("seq", "head"),
        P("seq", "head"),
        P("seq", "head"),
        P(),
        P(),
    )
    return jax.shard_map(
        on_device,
        mesh=mesh,
        in_specs=placed,
        out_specs=(P("seq", "head"), P("seq", "head"), P("seq", "head"), P("seq", "head")),
        check_vma=False,
    )
```

```python
import functools

import jax
import jax.numpy as jnp
from jax import lax
from jax.experimental import pallas as pl
from jax.experimental.pallas import tpu as pltpu
from jax.sharding import PartitionSpec as P

HEADS = 128
HEAD_DIM = 64
STATE = 128
GROUPS = 8
BLOCK = 256
CHUNK = 256
EXTRA = 16
VMEM_LIMIT = 60 * 1024 * 1024

F32 = jnp.float32
BF16 = jnp.bfloat16


def partner(block, axis, bit):
    count = lax.axis_size(axis)
    route = []
    for low in range(count):
        high = low | 1 << bit
        if high != low and high < count:
            route += [(low, high), (high, low)]
    return lax.ppermute(block, axis, route)


def dot_nn(a, b):
    return lax.dot_general(a, b, (((1,), (0,)), ((), ())), preferred_element_type=F32)


def dot_nt(a, b):
    return lax.dot_general(a, b, (((1,), (1,)), ((), ())), preferred_element_type=F32)


def dot_tn(a, b):
    return lax.dot_general(a, b, (((0,), (0,)), ((), ())), preferred_element_type=F32)


def iota(shape, dim):
    return lax.broadcasted_iota(jnp.int32, shape, dim)


def head_spread(heads, first_head, width):
    row = iota((heads, width), 0)
    return (row == first_head + iota((heads, width), 1) // HEAD_DIM).astype(F32).astype(BF16)


def head_spread_halves(heads, first_head, width):
    row = iota((2 * heads, width), 0)
    row = jnp.where(row >= heads, row - heads, row)
    return (row == first_head + iota((2 * heads, width), 1) // HEAD_DIM).astype(F32).astype(BF16)


def three_parts(value):
    high = value.astype(BF16)
    rest = value - high.astype(F32)
    mid = rest.astype(BF16)
    return high, mid, (rest - mid.astype(F32)).astype(BF16)


def spread_row(row, matrix):
    tall = jnp.broadcast_to(row, (8, row.shape[1]))
    return sum(dot_nn(part, matrix) for part in three_parts(tall))[0:1, :]


def token_setup(blocks, base, doc_ref, step_ref, rate_ref, e_ref, f_ref, whole_e_ref, whole_f_ref):
    heads = step_ref.shape[0]
    row, col = iota((heads, 2 * heads), 0), iota((heads, 2 * heads), 1)
    twice = ((row == col) | (row + heads == col)).astype(F32).astype(BF16)
    rate = spread_row(rate_ref[...], twice)
    row, col = iota((BLOCK, BLOCK), 0), iota((BLOCK, BLOCK), 1)
    lower = (row >= col).astype(F32).astype(BF16)
    eye = (row == col).astype(F32).astype(BF16)
    left = iota((BLOCK, 2 * heads), 1) < heads
    position = iota((BLOCK, 2 * heads), 0)

    def halves(value):
        top = value.astype(BF16).astype(F32)
        return jnp.where(left, top, value - top).astype(BF16)

    lead = jnp.ones((1, 2 * heads), F32)
    weights = []
    for k in range(blocks):
        rows = pl.ds(k * BLOCK, BLOCK)
        doc = doc_ref[base + k]
        step = step_ref[:, rows]
        parts = three_parts(jnp.concatenate([step, step], axis=0))
        cum = -rate * sum(dot_nt(lower, part) for part in parts)
        e = jnp.exp(cum)
        f = sum(dot_nt(eye, part) for part in parts) * jnp.exp(-cum)
        last = e[BLOCK - 1 : BLOCK, :]
        decay = jnp.where(doc == BLOCK, last, 0.0)
        e_ref[rows, :] = halves(e)
        f_ref[rows, :] = halves(f)
        whole_e_ref[rows, :] = halves(lead * jnp.where(position < doc, e, 0.0))
        lead = lead * decay
        weights.append((jnp.where(position >= doc, last * f, 0.0), decay))
    tail = jnp.ones((1, 2 * heads), F32)
    for k in reversed(range(blocks)):
        whole_f_ref[pl.ds(k * BLOCK, BLOCK), :] = halves(tail * weights[k][0])
        tail = tail * weights[k][1]


def summary(
    blocks, base, chunk, slot, lanes, doc_ref, x_ref, g_ref, b_ref, c_ref, e_ref, f_ref, msg_ref, pre_ref, suf_ref
):
    spread = head_spread_halves(e_ref.shape[1] // 2, chunk * (CHUNK // HEAD_DIM), CHUNK)
    position = iota((BLOCK, STATE), 0)
    ends, reads, decays, lasts = [], [], [], []
    for k in range(blocks):
        rows = pl.ds(k * BLOCK, BLOCK)
        doc = doc_ref[base + k]
        e_wide = dot_nn(e_ref[rows, :], spread)
        f_wide = dot_nn(f_ref[rows, :], spread)
        grad_in = (e_wide * g_ref[rows, :].astype(F32)).astype(BF16)
        data_in = (f_wide * x_ref[rows, :].astype(F32)).astype(BF16)
        write = jnp.where(position >= doc, b_ref[rows, :].astype(F32), 0.0).astype(BF16)
        read = jnp.where(position < doc, c_ref[rows, :].astype(F32), 0.0).astype(BF16)
        last = e_wide[BLOCK - 1 : BLOCK, :]
        ends.append(last * dot_tn(write, data_in))
        reads.append(dot_tn(read, grad_in))
        decays.append(jnp.where(doc == BLOCK, last, 0.0))
        lasts.append(last)
    state = jnp.zeros((STATE, CHUNK), F32)
    lead = jnp.ones((1, CHUNK), F32)
    for k in range(blocks):
        pre_ref[k, :, lanes] = state.astype(BF16)
        state = decays[k] * state + ends[k]
        lead = lead * decays[k]
    grad = jnp.zeros((STATE, CHUNK), F32)
    for k in reversed(range(blocks)):
        suf_ref[k, :, lanes] = (lasts[k] * grad).astype(BF16)
        grad = reads[k] + decays[k] * grad
    msg_ref[slot, :STATE, :] = state.astype(BF16)
    msg_ref[slot, STATE : 2 * STATE, :] = grad.astype(BF16)
    full = jnp.broadcast_to(lead, (EXTRA, CHUNK))
    top = full.astype(BF16).astype(F32)
    msg_ref[slot, 2 * STATE :, :] = jnp.where(iota((EXTRA, CHUNK), 0) == 0, top, full - top).astype(BF16)


def inner_block(
    doc, first_head, e, f, x_ref, g_ref, b_ref, c_ref, state, grad, skip_ref, y_ref, dx_ref, dw_ref, dr_ref
):
    heads = e.shape[1] // 2
    width = x_ref.shape[1]
    spread = head_spread_halves(heads, first_head, width)
    e_wide, f_wide = dot_nn(e, spread), dot_nn(f, spread)
    skip = spread_row(skip_ref[...], head_spread(heads, first_head, width))
    x, g = x_ref[...].astype(F32), g_ref[...].astype(F32)
    grad_in = (e_wide * g).astype(BF16)
    data_in = (f_wide * x).astype(BF16)
    position = iota((BLOCK, STATE), 0)
    b, c = b_ref[...], c_ref[...]
    write_on, read_on = position >= doc, position < doc
    write = jnp.where(write_on, b.astype(F32), 0.0).astype(BF16)
    read = jnp.where(read_on, c.astype(F32), 0.0).astype(BF16)
    row, col = iota((BLOCK, BLOCK), 0), iota((BLOCK, BLOCK), 1)
    keep = (row >= col) & ((row < doc) | (col >= doc))
    keep_t = (col >= row) & ((col < doc) | (row >= doc))
    score = jnp.where(keep, dot_nt(c, b), 0.0).astype(BF16)
    score_t = jnp.where(keep_t, dot_nt(b, c), 0.0).astype(BF16)
    y_ref[...] = (e_wide * (dot_nn(score, data_in) + dot_nn(read, state)) + skip * x).astype(BF16)
    dx_ref[...] = (f_wide * (dot_nn(score_t, grad_in) + dot_nn(write, grad)) + skip * g).astype(BF16)
    score_grad = jnp.where(keep, dot_nt(grad_in, data_in), 0.0).astype(BF16)
    dw_ref[...] = dot_tn(score_grad, c) + jnp.where(write_on, dot_nt(data_in, grad), 0.0)
    dr_ref[...] = dot_nn(score_grad, b) + jnp.where(read_on, dot_nt(grad_in, state), 0.0)


def summary_kernel(
    blocks, doc_ref, x_ref, g_ref, b_ref, c_ref, step_ref, rate_ref, msg_ref, pre_ref, suf_ref, e_ref, f_ref, we_ref, wf_ref
):
    chunk = pl.program_id(0)
    base = lax.axis_index("seq") * blocks

    @pl.when(chunk == 0)
    def _():
        token_setup(blocks, base, doc_ref, step_ref, rate_ref, e_ref, f_ref, we_ref, wf_ref)

    lanes = slice(None)
    summary(blocks, base, chunk, 0, lanes, doc_ref, x_ref, g_ref, b_ref, c_ref, e_ref, f_ref, msg_ref, pre_ref, suf_ref)


def inner_kernel(
    blocks, span, doc_ref, x_ref, g_ref, b_ref, c_ref, e_ref, f_ref, pre_ref, suf_ref, skip_ref, y_ref, dx_ref, dw_ref, dr_ref
):
    group, k = pl.program_id(0), pl.program_id(1)
    doc = doc_ref[lax.axis_index("seq") * blocks + k]
    inner_block(
        doc, group * span, e_ref[...], f_ref[...], x_ref, g_ref, b_ref, c_ref, pre_ref[0], suf_ref[0], skip_ref, y_ref, dx_ref, dw_ref, dr_ref
    )


def shard_at(place_ref, count, place):
    found = 0
    for shard in range(1, count):
        found = jnp.where(place_ref[shard] == place, shard, found)
    return found


def chain_kernel(count, order_ref, got_ref, out_ref):
    width = got_ref.shape[-1]

    def decay_of(shard):
        pair = got_ref[shard, 2 * STATE :, :].astype(F32)
        return pair[0:1, :] + pair[1:2, :]

    def forward(place, state):
        shard = order_ref[place]
        out_ref[shard, :STATE, :] = state.astype(BF16)
        return decay_of(shard) * state + got_ref[shard, :STATE, :].astype(F32)

    def backward(step, grad):
        shard = order_ref[count - 1 - step]
        out_ref[shard, STATE:, :] = grad.astype(BF16)
        return decay_of(shard) * grad + got_ref[shard, STATE : 2 * STATE, :].astype(F32)

    empty = jnp.zeros((STATE, width), F32)
    lax.fori_loop(0, count, forward, empty)
    lax.fori_loop(0, count, backward, empty)


def owner_at(step, count):
    return lax.rem(step, 2) * (count // 2) + step // 2


def exchange_kernel(
    blocks,
    span,
    groups,
    count,
    doc_ref,
    place_ref,
    x_ref,
    g_ref,
    b_ref,
    c_ref,
    step_ref,
    rate_ref,
    skip_ref,
    bx_ref,
    bg_ref,
    bb_ref,
    bc_ref,
    we_ref,
    wf_ref,
    dev_ref,
    y_ref,
    dx_ref,
    dw_ref,
    dr_ref,
    e_ref,
    f_ref,
    pre,
    suf,
    msg,
    got,
    chain,
    answer,
    back,
    send_sem,
    recv_sem,
    back_send_sem,
    back_recv_sem,
):
    step = pl.program_id(0)
    me = lax.axis_index("seq")
    base = me * blocks
    barrier = pltpu.get_barrier_semaphore()
    steps = count + groups * blocks

    def outward(owner, source):
        return pltpu.make_async_remote_copy(
            src_ref=msg.at[owner],
            dst_ref=got.at[source],
            send_sem=send_sem.at[owner],
            recv_sem=recv_sem.at[source],
            device_id={"seq": owner},
            device_id_type=pl.DeviceIdType.MESH,
        )

    def homeward(shard, source):
        return pltpu.make_async_remote_copy(
            src_ref=answer.at[shard],
            dst_ref=back.at[source],
            send_sem=back_send_sem.at[shard],
            recv_sem=back_recv_sem.at[source],
            device_id={"seq": shard},
            device_id_type=pl.DeviceIdType.MESH,
        )

    @pl.when(step == 0)
    def _():
        for ahead in range(1, count):
            pl.semaphore_signal(
                barrier,
                inc=1,
                device_id={"seq": lax.rem(me + ahead, count)},
                device_id_type=pl.DeviceIdType.MESH,
            )
        token_setup(blocks, base, doc_ref, step_ref, rate_ref, e_ref, f_ref, we_ref, wf_ref)

    @pl.when(step < count)
    def _():
        owner = owner_at(step, count)
        lanes = pl.ds(pl.multiple_of(owner * CHUNK, CHUNK), CHUNK)
        summary(
            blocks, base, owner, owner, lanes, doc_ref, x_ref, g_ref, b_ref, c_ref, e_ref, f_ref, msg, pre, suf
        )

        @pl.when(step == 0)
        def _():
            pl.semaphore_wait(barrier, count - 1)

        @pl.when(owner != me)
        def _():
            outward(owner, me).start()

        @pl.when(owner == me)
        def _():
            got[me] = msg[owner]

    @pl.when((step >= count) & (step < steps))
    def _():
        group = (step - count) // blocks
        k = lax.rem(step - count, blocks)
        rows = pl.ds(pl.multiple_of(k * BLOCK, BLOCK), BLOCK)
        wide = span * HEAD_DIM
        lanes = pl.ds(pl.multiple_of(group * wide, wide), wide)
        inner_block(
            doc_ref[base + k],
            group * span,
            e_ref[rows, :],
            f_ref[rows, :],
            bx_ref,
            bg_ref,
            bb_ref,
            bc_ref,
            pre[k, :, lanes],
            suf[k, :, lanes],
            skip_ref,
            y_ref,
            dx_ref,
            dw_ref,
            dr_ref,
        )

    half = count // 2
    turn = 2 * lax.rem(me, half) + me // half
    early = half + 1
    chain_step = early + (turn * (steps - 1 - early)) // (count - 1)

    @pl.when(step == chain_step)
    def _():
        for shard in range(count):

            @pl.when(me != shard)
            def _():
                outward(shard, shard).wait_recv()

        def decay_of(shard):
            pair = got[shard, 2 * STATE :, :].astype(F32)
            return pair[0:1, :] + pair[1:2, :]

        order = [shard_at(place_ref, count, place) for place in range(count)]
        state = jnp.zeros((STATE, CHUNK), F32)
        for place in range(count):
            shard = order[place]
            chain[place, :STATE, :] = state.astype(BF16)
            state = decay_of(shard) * state + got[shard, :STATE, :].astype(F32)
        grad = jnp.zeros((STATE, CHUNK), F32)
        for place in reversed(range(count)):
            shard = order[place]
            chain[place, STATE:, :] = grad.astype(BF16)
            grad = decay_of(shard) * grad + got[shard, STATE : 2 * STATE, :].astype(F32)
        for shard in range(count):
            answer[shard] = chain[place_ref[shard]]

            @pl.when(me != shard)
            def _():
                homeward(shard, me).start()

        back[me] = answer[me]

    @pl.when(step == steps)
    def _():
        for shard in range(count):

            @pl.when(me != shard)
            def _():
                homeward(shard, shard).wait_recv()

        for shard in range(count):

            @pl.when(me != shard)
            def _():
                outward(shard, me).wait_send()
                homeward(shard, me).wait_send()

        dev_ref[...] = back[...]


def finish_kernel(
    span, x_ref, g_ref, b_ref, c_ref, e_ref, f_ref, dev_ref, yp_ref, dxp_ref, dwp_ref, drp_ref, y_ref, dx_ref, dw_ref, dr_ref
):
    spread = head_spread_halves(e_ref.shape[1] // 2, pl.program_id(0) * span, span * HEAD_DIM)
    e_wide = dot_nn(e_ref[...], spread)
    f_wide = dot_nn(f_ref[...], spread)
    grad_in = (e_wide * g_ref[...].astype(F32)).astype(BF16)
    data_in = (f_wide * x_ref[...].astype(F32)).astype(BF16)
    parts = range(dev_ref.shape[0])
    state = jnp.concatenate([dev_ref[j, :STATE, :] for j in parts], axis=1)
    grad = jnp.concatenate([dev_ref[j, STATE:, :] for j in parts], axis=1)
    y_ref[...] = (yp_ref[...].astype(F32) + e_wide * dot_nn(c_ref[...], state)).astype(BF16)
    dx_ref[...] = (dxp_ref[...].astype(F32) + f_wide * dot_nn(b_ref[...], grad)).astype(BF16)
    dw_ref[...] = dwp_ref[...] + dot_nt(data_in, grad)
    dr_ref[...] = drp_ref[...] + dot_nt(grad_in, state)


def on_device(
    seq_input,
    step_size,
    decay_rate,
    skip_gain,
    state_write,
    state_read,
    out_grad,
    segment_order,
    doc_start,
):
    heads = decay_rate.shape[0]
    group_heads = HEADS // GROUPS
    span = min(heads, group_heads)
    groups = heads // span
    group_devices = max(1, group_heads // heads)
    levels = group_devices.bit_length() - 1
    tokens = seq_input.shape[0]
    blocks = tokens // BLOCK
    channels = heads * HEAD_DIM
    chunks = channels // CHUNK
    group_chunks = chunks // groups
    seq_count = lax.axis_size("seq")
    head_rank = lax.axis_index("head")
    own_write, own_read = (state_write, state_read)
    for level in range(levels):
        other_write, other_read = partner((own_write, own_read), "head", level)
        upper_half = head_rank >> level & 1 == 1
        own_write = jnp.where(
            upper_half,
            jnp.concatenate([other_write, own_write], 1),
            jnp.concatenate([own_write, other_write], 1),
        )
        own_read = jnp.where(
            upper_half,
            jnp.concatenate([other_read, own_read], 1),
            jnp.concatenate([own_read, other_read], 1),
        )
    rate_row = decay_rate.reshape(1, heads)
    skip_row = skip_gain.reshape(1, heads)
    smem = pl.BlockSpec(memory_space=pltpu.SMEM)
    params = pltpu.CompilerParams(vmem_limit_bytes=VMEM_LIMIT)
    rows = 2 * STATE + EXTRA
    lanes = span * HEAD_DIM
    column_shape = jax.ShapeDtypeStruct((tokens, 2 * heads), BF16)
    part_shapes = (
        jax.ShapeDtypeStruct((tokens, channels), BF16),
        jax.ShapeDtypeStruct((tokens, channels), BF16),
        jax.ShapeDtypeStruct((tokens, groups * STATE), F32),
        jax.ShapeDtypeStruct((tokens, groups * STATE), F32),
    )

    def whole_spec(shape):
        return pl.BlockSpec(shape, lambda *place: (0,) * len(shape))

    def part_specs(where):
        return (
            pl.BlockSpec((BLOCK, lanes), where),
            pl.BlockSpec((BLOCK, lanes), where),
            pl.BlockSpec((BLOCK, STATE), where),
            pl.BlockSpec((BLOCK, STATE), where),
        )

    def chunk_specs(chunk_of):
        return [
            pl.BlockSpec((tokens, CHUNK), lambda i: (0, chunk_of(i))),
            pl.BlockSpec((tokens, CHUNK), lambda i: (0, chunk_of(i))),
            pl.BlockSpec((tokens, STATE), lambda i: (0, chunk_of(i) // group_chunks)),
            pl.BlockSpec((tokens, STATE), lambda i: (0, chunk_of(i) // group_chunks)),
        ]

    def by_block(g, k):
        return (k, g)

    tables = [whole_spec((heads, tokens)), whole_spec((1, heads))]
    if chunks == seq_count:

        def served(i):
            return owner_at(jnp.minimum(i, chunks - 1), chunks)

        def block_of(i):
            place = jnp.clip(i - chunks, 0, groups * blocks - 1)
            return (lax.rem(place, blocks), place // blocks)

        whole_e, whole_f, device, *parts = pl.pallas_call(
            functools.partial(exchange_kernel, blocks, span, groups, seq_count),
            grid=(chunks + groups * blocks + 1,),
            out_shape=(
                column_shape,
                column_shape,
                jax.ShapeDtypeStruct((chunks, 2 * STATE, CHUNK), BF16),
                *part_shapes,
            ),
            in_specs=[smem, smem, *chunk_specs(served), *tables, whole_spec((1, heads)), *part_specs(block_of)],
            out_specs=(
                whole_spec((tokens, 2 * heads)),
                whole_spec((tokens, 2 * heads)),
                whole_spec((chunks, 2 * STATE, CHUNK)),
                *part_specs(block_of),
            ),
            scratch_shapes=[
                pltpu.VMEM((tokens, 2 * heads), BF16),
                pltpu.VMEM((tokens, 2 * heads), BF16),
                pltpu.VMEM((blocks, STATE, channels), BF16),
                pltpu.VMEM((blocks, STATE, channels), BF16),
                pltpu.VMEM((chunks, rows, CHUNK), BF16),
                pltpu.VMEM((chunks, rows, CHUNK), BF16),
                pltpu.VMEM((chunks, 2 * STATE, CHUNK), BF16),
                pltpu.VMEM((chunks, 2 * STATE, CHUNK), BF16),
                pltpu.VMEM((chunks, 2 * STATE, CHUNK), BF16),
                pltpu.SemaphoreType.DMA((chunks,)),
                pltpu.SemaphoreType.DMA((chunks,)),
                pltpu.SemaphoreType.DMA((chunks,)),
                pltpu.SemaphoreType.DMA((chunks,)),
            ],
            compiler_params=pltpu.CompilerParams(
                vmem_limit_bytes=VMEM_LIMIT, collective_id=0, has_side_effects=True
            ),
            name="exchange",
        )(
            doc_start,
            segment_order,
            seq_input,
            out_grad,
            own_write,
            own_read,
            step_size,
            rate_row,
            skip_row,
            seq_input,
            out_grad,
            own_write,
            own_read,
        )
    else:
        state_shape = jax.ShapeDtypeStruct((blocks, STATE, channels), BF16)
        message, pre, suf, e_cols, f_cols, whole_e, whole_f = pl.pallas_call(
            functools.partial(summary_kernel, blocks),
            grid=(chunks,),
            out_shape=(
                jax.ShapeDtypeStruct((chunks, rows, CHUNK), BF16),
                state_shape,
                state_shape,
                *[column_shape] * 4,
            ),
            in_specs=[smem, *chunk_specs(lambda i: i), *tables],
            out_specs=(
                pl.BlockSpec((1, rows, CHUNK), lambda i: (i, 0, 0)),
                pl.BlockSpec((blocks, STATE, CHUNK), lambda i: (0, 0, i)),
                pl.BlockSpec((blocks, STATE, CHUNK), lambda i: (0, 0, i)),
                *[whole_spec((tokens, 2 * heads))] * 4,
            ),
            compiler_params=params,
            name="summary",
        )(doc_start, seq_input, out_grad, own_write, own_read, step_size, rate_row)
        width = channels // seq_count
        message = jnp.transpose(message, (1, 0, 2)).reshape(rows, seq_count, width)
        message = jnp.transpose(message, (1, 0, 2))
        got = lax.all_to_all(message, "seq", split_axis=0, concat_axis=0, tiled=True)
        parts = pl.pallas_call(
            functools.partial(inner_kernel, blocks, span),
            grid=(groups, blocks),
            out_shape=part_shapes,
            in_specs=[
                smem,
                *part_specs(by_block),
                pl.BlockSpec((BLOCK, 2 * heads), lambda g, k: (k, 0)),
                pl.BlockSpec((BLOCK, 2 * heads), lambda g, k: (k, 0)),
                pl.BlockSpec((1, STATE, lanes), lambda g, k: (k, 0, g)),
                pl.BlockSpec((1, STATE, lanes), lambda g, k: (k, 0, g)),
                whole_spec((1, heads)),
            ],
            out_specs=part_specs(by_block),
            compiler_params=params,
            name="inner",
        )(doc_start, seq_input, out_grad, own_write, own_read, e_cols, f_cols, pre, suf, skip_row)
        order = jnp.zeros((seq_count,), jnp.int32).at[segment_order].set(
            jnp.arange(seq_count, dtype=jnp.int32)
        )
        answer = pl.pallas_call(
            functools.partial(chain_kernel, seq_count),
            out_shape=jax.ShapeDtypeStruct((seq_count, 2 * STATE, width), BF16),
            in_specs=[smem, pl.BlockSpec(memory_space=pltpu.VMEM)],
            out_specs=pl.BlockSpec(memory_space=pltpu.VMEM),
            compiler_params=params,
            name="chain",
        )(order, got)
        device = lax.all_to_all(answer, "seq", split_axis=0, concat_axis=0, tiled=True)
        device = jnp.transpose(device, (1, 0, 2)).reshape(2 * STATE, chunks, CHUNK)
        device = jnp.transpose(device, (1, 0, 2))

    mixed, input_grad, write_sum, read_sum = pl.pallas_call(
        functools.partial(finish_kernel, span),
        grid=(groups, blocks),
        out_shape=part_shapes,
        in_specs=[
            *part_specs(by_block),
            pl.BlockSpec((BLOCK, 2 * heads), lambda g, k: (k, 0)),
            pl.BlockSpec((BLOCK, 2 * heads), lambda g, k: (k, 0)),
            pl.BlockSpec((group_chunks, 2 * STATE, CHUNK), lambda g, k: (g, 0, 0)),
            *part_specs(by_block),
        ],
        out_specs=part_specs(by_block),
        compiler_params=params,
        name="finish",
    )(seq_input, out_grad, own_write, own_read, whole_e, whole_f, device, *parts)

    for level in range(levels):
        other_write_sum, other_read_sum = partner(
            (write_sum.astype(BF16), read_sum.astype(BF16)), "head", level
        )
        write_sum = write_sum + other_write_sum.astype(F32)
        read_sum = read_sum + other_read_sum.astype(F32)
    own_width = groups * STATE // group_devices
    if group_devices > 1:
        own_first = head_rank % group_devices * own_width
        write_sum = lax.dynamic_slice_in_dim(write_sum, own_first, own_width, 1)
        read_sum = lax.dynamic_slice_in_dim(read_sum, own_first, own_width, 1)
    return mixed, input_grad, write_sum, read_sum


def solution(mesh):
    placed = (
        P("seq", "head"),
        P("head", "seq"),
        P("head"),
        P("head"),
        P("seq", "head"),
        P("seq", "head"),
        P("seq", "head"),
        P(),
        P(),
    )
    return jax.shard_map(
        on_device,
        mesh=mesh,
        in_specs=placed,
        out_specs=(P("seq", "head"), P("seq", "head"), P("seq", "head"), P("seq", "head")),
        check_vma=False,
    )
```

```python
import functools

import jax
import jax.numpy as jnp
from jax import lax
from jax.experimental import pallas as pl
from jax.experimental.pallas import tpu as pltpu
from jax.sharding import PartitionSpec as P

HEADS = 128
HEAD_DIM = 64
STATE = 128
GROUPS = 8
BLOCK = 256
CHUNK = 256
EXTRA = 16
VMEM_LIMIT = 60 * 1024 * 1024

F32 = jnp.float32
BF16 = jnp.bfloat16


def partner(block, axis, bit):
    count = lax.axis_size(axis)
    route = []
    for low in range(count):
        high = low | 1 << bit
        if high != low and high < count:
            route += [(low, high), (high, low)]
    return lax.ppermute(block, axis, route)


def dot_nn(a, b):
    return lax.dot_general(a, b, (((1,), (0,)), ((), ())), preferred_element_type=F32)


def dot_nt(a, b):
    return lax.dot_general(a, b, (((1,), (1,)), ((), ())), preferred_element_type=F32)


def dot_tn(a, b):
    return lax.dot_general(a, b, (((0,), (0,)), ((), ())), preferred_element_type=F32)


def iota(shape, dim):
    return lax.broadcasted_iota(jnp.int32, shape, dim)


def head_spread(heads, first_head, width):
    row = iota((heads, width), 0)
    return (row == first_head + iota((heads, width), 1) // HEAD_DIM).astype(F32).astype(BF16)


def head_spread_halves(heads, first_head, width):
    row = iota((2 * heads, width), 0)
    row = jnp.where(row >= heads, row - heads, row)
    return (row == first_head + iota((2 * heads, width), 1) // HEAD_DIM).astype(F32).astype(BF16)


def three_parts(value):
    high = value.astype(BF16)
    rest = value - high.astype(F32)
    mid = rest.astype(BF16)
    return high, mid, (rest - mid.astype(F32)).astype(BF16)


def spread_row(row, matrix):
    tall = jnp.broadcast_to(row, (8, row.shape[1]))
    return sum(dot_nn(part, matrix) for part in three_parts(tall))[0:1, :]


def token_setup(blocks, base, doc_ref, step_ref, rate_ref, e_ref, f_ref, whole_e_ref, whole_f_ref):
    heads = step_ref.shape[0]
    row, col = iota((heads, 2 * heads), 0), iota((heads, 2 * heads), 1)
    twice = ((row == col) | (row + heads == col)).astype(F32).astype(BF16)
    rate = spread_row(rate_ref[...], twice)
    row, col = iota((BLOCK, BLOCK), 0), iota((BLOCK, BLOCK), 1)
    lower = (row >= col).astype(F32).astype(BF16)
    eye = (row == col).astype(F32).astype(BF16)
    left = iota((BLOCK, 2 * heads), 1) < heads
    position = iota((BLOCK, 2 * heads), 0)

    def halves(value):
        top = value.astype(BF16).astype(F32)
        return jnp.where(left, top, value - top).astype(BF16)

    lead = jnp.ones((1, 2 * heads), F32)
    weights = []
    for k in range(blocks):
        rows = pl.ds(k * BLOCK, BLOCK)
        doc = doc_ref[base + k]
        step = step_ref[:, rows]
        parts = three_parts(jnp.concatenate([step, step], axis=0))
        cum = -rate * sum(dot_nt(lower, part) for part in parts)
        e = jnp.exp(cum)
        f = sum(dot_nt(eye, part) for part in parts) * jnp.exp(-cum)
        last = e[BLOCK - 1 : BLOCK, :]
        decay = jnp.where(doc == BLOCK, last, 0.0)
        e_ref[rows, :] = halves(e)
        f_ref[rows, :] = halves(f)
        whole_e_ref[rows, :] = halves(lead * jnp.where(position < doc, e, 0.0))
        lead = lead * decay
        weights.append((jnp.where(position >= doc, last * f, 0.0), decay))
    tail = jnp.ones((1, 2 * heads), F32)
    for k in reversed(range(blocks)):
        whole_f_ref[pl.ds(k * BLOCK, BLOCK), :] = halves(tail * weights[k][0])
        tail = tail * weights[k][1]


def summary(
    blocks, base, chunk, slot, lanes, doc_ref, x_ref, g_ref, b_ref, c_ref, e_ref, f_ref, msg_ref, pre_ref, suf_ref, scale_ref
):
    spread = head_spread_halves(e_ref.shape[1] // 2, chunk * (CHUNK // HEAD_DIM), CHUNK)
    position = iota((BLOCK, STATE), 0)
    ends, reads, decays, lasts = [], [], [], []
    for k in range(blocks):
        rows = pl.ds(k * BLOCK, BLOCK)
        doc = doc_ref[base + k]
        e_wide = dot_nn(e_ref[rows, :], spread)
        f_wide = dot_nn(f_ref[rows, :], spread)
        grad_in = (e_wide * g_ref[rows, :].astype(F32)).astype(BF16)
        data_in = (f_wide * x_ref[rows, :].astype(F32)).astype(BF16)
        write = jnp.where(position >= doc, b_ref[rows, :].astype(F32), 0.0).astype(BF16)
        read = jnp.where(position < doc, c_ref[rows, :].astype(F32), 0.0).astype(BF16)
        last = e_wide[BLOCK - 1 : BLOCK, :]
        ends.append(last * dot_tn(write, data_in))
        reads.append(dot_tn(read, grad_in))
        decays.append(jnp.where(doc == BLOCK, last, 0.0))
        lasts.append(last)
    state = jnp.zeros((STATE, CHUNK), F32)
    lead = jnp.ones((1, CHUNK), F32)
    for k in range(blocks):
        pre_ref[k, :, lanes] = state.astype(BF16)
        scale_ref[k, 0:8, lanes] = jnp.broadcast_to(lead, (8, CHUNK))
        state = decays[k] * state + ends[k]
        lead = lead * decays[k]
    grad = jnp.zeros((STATE, CHUNK), F32)
    tail = jnp.ones((1, CHUNK), F32)
    for k in reversed(range(blocks)):
        suf_ref[k, :, lanes] = (lasts[k] * grad).astype(BF16)
        scale_ref[k, 8:16, lanes] = jnp.broadcast_to(lasts[k] * tail, (8, CHUNK))
        grad = reads[k] + decays[k] * grad
        tail = tail * decays[k]
    msg_ref[slot, :STATE, :] = state.astype(BF16)
    msg_ref[slot, STATE : 2 * STATE, :] = grad.astype(BF16)
    full = jnp.broadcast_to(lead, (EXTRA, CHUNK))
    top = full.astype(BF16).astype(F32)
    msg_ref[slot, 2 * STATE :, :] = jnp.where(iota((EXTRA, CHUNK), 0) == 0, top, full - top).astype(BF16)


def inner_block(
    doc, first_head, e, f, x_ref, g_ref, b_ref, c_ref, state, grad, skip_ref, y_ref, dx_ref, dw_ref, dr_ref
):
    heads = e.shape[1] // 2
    width = x_ref.shape[1]
    spread = head_spread_halves(heads, first_head, width)
    e_wide, f_wide = dot_nn(e, spread), dot_nn(f, spread)
    skip = spread_row(skip_ref[...], head_spread(heads, first_head, width))
    x, g = x_ref[...].astype(F32), g_ref[...].astype(F32)
    grad_in = (e_wide * g).astype(BF16)
    data_in = (f_wide * x).astype(BF16)
    position = iota((BLOCK, STATE), 0)
    b, c = b_ref[...], c_ref[...]
    write_on, read_on = position >= doc, position < doc
    write = jnp.where(write_on, b.astype(F32), 0.0).astype(BF16)
    read = jnp.where(read_on, c.astype(F32), 0.0).astype(BF16)
    row, col = iota((BLOCK, BLOCK), 0), iota((BLOCK, BLOCK), 1)
    keep = (row >= col) & ((row < doc) | (col >= doc))
    keep_t = (col >= row) & ((col < doc) | (row >= doc))
    score = jnp.where(keep, dot_nt(c, b), 0.0).astype(BF16)
    score_t = jnp.where(keep_t, dot_nt(b, c), 0.0).astype(BF16)
    y_ref[...] = (e_wide * (dot_nn(score, data_in) + dot_nn(read, state)) + skip * x).astype(BF16)
    dx_ref[...] = (f_wide * (dot_nn(score_t, grad_in) + dot_nn(write, grad)) + skip * g).astype(BF16)
    score_grad = jnp.where(keep, dot_nt(grad_in, data_in), 0.0).astype(BF16)
    dw_ref[...] = dot_tn(score_grad, c) + jnp.where(write_on, dot_nt(data_in, grad), 0.0)
    dr_ref[...] = dot_nn(score_grad, b) + jnp.where(read_on, dot_nt(grad_in, state), 0.0)


def summary_kernel(
    blocks, doc_ref, x_ref, g_ref, b_ref, c_ref, step_ref, rate_ref, msg_ref, pre_ref, suf_ref, e_ref, f_ref, we_ref, wf_ref, scale
):
    chunk = pl.program_id(0)
    base = lax.axis_index("seq") * blocks

    @pl.when(chunk == 0)
    def _():
        token_setup(blocks, base, doc_ref, step_ref, rate_ref, e_ref, f_ref, we_ref, wf_ref)

    lanes = slice(None)
    summary(blocks, base, chunk, 0, lanes, doc_ref, x_ref, g_ref, b_ref, c_ref, e_ref, f_ref, msg_ref, pre_ref, suf_ref, scale)


def inner_kernel(
    blocks, span, doc_ref, x_ref, g_ref, b_ref, c_ref, e_ref, f_ref, pre_ref, suf_ref, skip_ref, y_ref, dx_ref, dw_ref, dr_ref
):
    group, k = pl.program_id(0), pl.program_id(1)
    doc = doc_ref[lax.axis_index("seq") * blocks + k]
    inner_block(
        doc, group * span, e_ref[...], f_ref[...], x_ref, g_ref, b_ref, c_ref, pre_ref[0], suf_ref[0], skip_ref, y_ref, dx_ref, dw_ref, dr_ref
    )


def shard_at(place_ref, count, place):
    found = 0
    for shard in range(1, count):
        found = jnp.where(place_ref[shard] == place, shard, found)
    return found


def chain_kernel(count, order_ref, got_ref, out_ref):
    width = got_ref.shape[-1]

    def decay_of(shard):
        pair = got_ref[shard, 2 * STATE :, :].astype(F32)
        return pair[0:1, :] + pair[1:2, :]

    def forward(place, state):
        shard = order_ref[place]
        out_ref[shard, :STATE, :] = state.astype(BF16)
        return decay_of(shard) * state + got_ref[shard, :STATE, :].astype(F32)

    def backward(step, grad):
        shard = order_ref[count - 1 - step]
        out_ref[shard, STATE:, :] = grad.astype(BF16)
        return decay_of(shard) * grad + got_ref[shard, STATE : 2 * STATE, :].astype(F32)

    empty = jnp.zeros((STATE, width), F32)
    lax.fori_loop(0, count, forward, empty)
    lax.fori_loop(0, count, backward, empty)


def owner_of(chunk, groups, count):
    each = count // groups
    return lax.rem(chunk, each) * groups + chunk // each


def exchange_kernel(
    blocks,
    span,
    groups,
    count,
    doc_ref,
    place_ref,
    x_ref,
    g_ref,
    b_ref,
    c_ref,
    step_ref,
    rate_ref,
    skip_ref,
    bx_ref,
    bg_ref,
    bb_ref,
    bc_ref,
    we_ref,
    wf_ref,
    dev_ref,
    y_ref,
    dx_ref,
    dw_ref,
    dr_ref,
    e_ref,
    f_ref,
    pre,
    suf,
    scale,
    msg,
    got,
    chain,
    answer,
    back,
    send_sem,
    recv_sem,
    back_send_sem,
    back_recv_sem,
):
    step = pl.program_id(0)
    me = lax.axis_index("seq")
    base = me * blocks
    barrier = pltpu.get_barrier_semaphore()
    steps = count + groups * blocks

    def outward(chunk, source):
        return pltpu.make_async_remote_copy(
            src_ref=msg.at[chunk],
            dst_ref=got.at[source],
            send_sem=send_sem.at[chunk],
            recv_sem=recv_sem.at[source],
            device_id={"seq": owner_of(chunk, groups, count)},
            device_id_type=pl.DeviceIdType.MESH,
        )

    def homeward(shard, chunk):
        return pltpu.make_async_remote_copy(
            src_ref=answer.at[shard],
            dst_ref=back.at[chunk],
            send_sem=back_send_sem.at[shard],
            recv_sem=back_recv_sem.at[chunk],
            device_id={"seq": shard},
            device_id_type=pl.DeviceIdType.MESH,
        )

    each = count // groups
    mine = lax.rem(me, groups) * each + me // groups

    @pl.when(step == 0)
    def _():
        for ahead in range(1, count):
            pl.semaphore_signal(
                barrier,
                inc=1,
                device_id={"seq": lax.rem(me + ahead, count)},
                device_id_type=pl.DeviceIdType.MESH,
            )
        token_setup(blocks, base, doc_ref, step_ref, rate_ref, e_ref, f_ref, we_ref, wf_ref)

    @pl.when(step < count)
    def _():
        lanes = pl.ds(pl.multiple_of(step * CHUNK, CHUNK), CHUNK)
        summary(
            blocks, base, step, step, lanes, doc_ref, x_ref, g_ref, b_ref, c_ref, e_ref, f_ref, msg, pre, suf, scale
        )

        @pl.when(step == 0)
        def _():
            pl.semaphore_wait(barrier, count - 1)

        @pl.when(step != mine)
        def _():
            outward(step, me).start()

        @pl.when(step == mine)
        def _():
            got[me] = msg[step]

    full_step = count + blocks
    chain_step = jnp.where(
        mine >= count - each, full_step, jnp.minimum(count // 2 + 1 + mine, full_step)
    )

    @pl.when(step == chain_step)
    def _():
        for shard in range(count):

            @pl.when(me != shard)
            def _():
                outward((shard % groups) * each + shard // groups, shard).wait_recv()

        def decay_of(shard):
            pair = got[shard, 2 * STATE :, :].astype(F32)
            return pair[0:1, :] + pair[1:2, :]

        order = [shard_at(place_ref, count, place) for place in range(count)]
        state = jnp.zeros((STATE, CHUNK), F32)
        for place in range(count):
            shard = order[place]
            chain[place, :STATE, :] = state.astype(BF16)
            state = decay_of(shard) * state + got[shard, :STATE, :].astype(F32)
        grad = jnp.zeros((STATE, CHUNK), F32)
        for place in reversed(range(count)):
            shard = order[place]
            chain[place, STATE:, :] = grad.astype(BF16)
            grad = decay_of(shard) * grad + got[shard, STATE : 2 * STATE, :].astype(F32)
        for shard in range(count):
            answer[shard] = chain[place_ref[shard]]

            @pl.when(me != shard)
            def _():
                homeward(shard, mine).start()

        back[mine] = answer[me]

    def wait_back(first, last):
        for chunk in range(first, last):

            @pl.when(mine != chunk)
            def _():
                homeward((chunk % each) * groups + chunk // each, chunk).wait_recv()

    wide = span * HEAD_DIM

    def run_block(state, grad, group, k, rows):
        inner_block(
            doc_ref[base + k],
            group * span,
            e_ref[rows, :],
            f_ref[rows, :],
            bx_ref,
            bg_ref,
            bb_ref,
            bc_ref,
            state,
            grad,
            skip_ref,
            y_ref,
            dx_ref,
            dw_ref,
            dr_ref,
        )

    @pl.when((step >= count) & (step < full_step))
    def _():
        k = step - count
        rows = pl.ds(pl.multiple_of(k * BLOCK, BLOCK), BLOCK)
        lanes = pl.ds((groups - 1) * wide, wide)
        run_block(pre[k, :, lanes], suf[k, :, lanes], groups - 1, k, rows)

    if groups > 1:

        @pl.when(step == full_step)
        def _():
            wait_back(0, count - each)

        @pl.when((step >= full_step) & (step < steps))
        def _():
            group = (step - full_step) // blocks
            k = lax.rem(step - full_step, blocks)
            rows = pl.ds(pl.multiple_of(k * BLOCK, BLOCK), BLOCK)
            lanes = pl.ds(pl.multiple_of(group * wide, wide), wide)
            chunks = [back[group * each + j] for j in range(each)]
            state_in = jnp.concatenate([part[:STATE] for part in chunks], axis=1)
            grad_in = jnp.concatenate([part[STATE:] for part in chunks], axis=1)
            lead, tail = scale[k, 0:1, lanes], scale[k, 8:9, lanes]
            state = pre[k, :, lanes].astype(F32) + lead * state_in.astype(F32)
            grad = suf[k, :, lanes].astype(F32) + tail * grad_in.astype(F32)
            run_block(state.astype(BF16), grad.astype(BF16), group, k, rows)

    @pl.when(step == steps)
    def _():
        wait_back(count - each, count)
        for chunk in range(count):

            @pl.when(mine != chunk)
            def _():
                outward(chunk, me).wait_send()

        for shard in range(count):

            @pl.when(me != shard)
            def _():
                homeward(shard, mine).wait_send()

        for j in range(each):
            dev_ref[j] = back[count - each + j]


def finish_kernel(
    span, done, x_ref, g_ref, b_ref, c_ref, e_ref, f_ref, dev_ref, yp_ref, dxp_ref, dwp_ref, drp_ref, y_ref, dx_ref, dw_ref, dr_ref
):
    group = pl.program_id(0)

    @pl.when(group < done)
    def _():
        y_ref[...] = yp_ref[...]
        dx_ref[...] = dxp_ref[...]
        dw_ref[...] = dwp_ref[...]
        dr_ref[...] = drp_ref[...]

    @pl.when(group >= done)
    def _():
        spread = head_spread_halves(e_ref.shape[1] // 2, group * span, span * HEAD_DIM)
        e_wide = dot_nn(e_ref[...], spread)
        f_wide = dot_nn(f_ref[...], spread)
        grad_in = (e_wide * g_ref[...].astype(F32)).astype(BF16)
        data_in = (f_wide * x_ref[...].astype(F32)).astype(BF16)
        parts = range(dev_ref.shape[0])
        state = jnp.concatenate([dev_ref[j, :STATE, :] for j in parts], axis=1)
        grad = jnp.concatenate([dev_ref[j, STATE:, :] for j in parts], axis=1)
        y_ref[...] = (yp_ref[...].astype(F32) + e_wide * dot_nn(c_ref[...], state)).astype(BF16)
        dx_ref[...] = (dxp_ref[...].astype(F32) + f_wide * dot_nn(b_ref[...], grad)).astype(BF16)
        dw_ref[...] = dwp_ref[...] + dot_nt(data_in, grad)
        dr_ref[...] = drp_ref[...] + dot_nt(grad_in, state)


def on_device(
    seq_input,
    step_size,
    decay_rate,
    skip_gain,
    state_write,
    state_read,
    out_grad,
    segment_order,
    doc_start,
):
    heads = decay_rate.shape[0]
    group_heads = HEADS // GROUPS
    span = min(heads, group_heads)
    groups = heads // span
    group_devices = max(1, group_heads // heads)
    levels = group_devices.bit_length() - 1
    tokens = seq_input.shape[0]
    blocks = tokens // BLOCK
    channels = heads * HEAD_DIM
    chunks = channels // CHUNK
    group_chunks = chunks // groups
    seq_count = lax.axis_size("seq")
    head_rank = lax.axis_index("head")
    own_write, own_read = (state_write, state_read)
    for level in range(levels):
        other_write, other_read = partner((own_write, own_read), "head", level)
        upper_half = head_rank >> level & 1 == 1
        own_write = jnp.where(
            upper_half,
            jnp.concatenate([other_write, own_write], 1),
            jnp.concatenate([own_write, other_write], 1),
        )
        own_read = jnp.where(
            upper_half,
            jnp.concatenate([other_read, own_read], 1),
            jnp.concatenate([own_read, other_read], 1),
        )
    rate_row = decay_rate.reshape(1, heads)
    skip_row = skip_gain.reshape(1, heads)
    smem = pl.BlockSpec(memory_space=pltpu.SMEM)
    params = pltpu.CompilerParams(vmem_limit_bytes=VMEM_LIMIT)
    rows = 2 * STATE + EXTRA
    lanes = span * HEAD_DIM
    column_shape = jax.ShapeDtypeStruct((tokens, 2 * heads), BF16)
    part_shapes = (
        jax.ShapeDtypeStruct((tokens, channels), BF16),
        jax.ShapeDtypeStruct((tokens, channels), BF16),
        jax.ShapeDtypeStruct((tokens, groups * STATE), F32),
        jax.ShapeDtypeStruct((tokens, groups * STATE), F32),
    )

    def whole_spec(shape):
        return pl.BlockSpec(shape, lambda *place: (0,) * len(shape))

    def part_specs(where):
        return (
            pl.BlockSpec((BLOCK, lanes), where),
            pl.BlockSpec((BLOCK, lanes), where),
            pl.BlockSpec((BLOCK, STATE), where),
            pl.BlockSpec((BLOCK, STATE), where),
        )

    def chunk_specs(chunk_of):
        return [
            pl.BlockSpec((tokens, CHUNK), lambda i: (0, chunk_of(i))),
            pl.BlockSpec((tokens, CHUNK), lambda i: (0, chunk_of(i))),
            pl.BlockSpec((tokens, STATE), lambda i: (0, chunk_of(i) // group_chunks)),
            pl.BlockSpec((tokens, STATE), lambda i: (0, chunk_of(i) // group_chunks)),
        ]

    def by_block(g, k):
        return (k, g)

    tables = [whole_spec((heads, tokens)), whole_spec((1, heads))]
    if chunks == seq_count:

        done = groups - 1

        def served(i):
            return jnp.minimum(i, chunks - 1)

        def block_of(i):
            place = jnp.clip(i - chunks, 0, groups * blocks - 1)
            return (lax.rem(place, blocks), lax.rem(place // blocks + groups - 1, groups))

        whole_e, whole_f, device, *parts = pl.pallas_call(
            functools.partial(exchange_kernel, blocks, span, groups, seq_count),
            grid=(chunks + groups * blocks + 1,),
            out_shape=(
                column_shape,
                column_shape,
                jax.ShapeDtypeStruct((group_chunks, 2 * STATE, CHUNK), BF16),
                *part_shapes,
            ),
            in_specs=[smem, smem, *chunk_specs(served), *tables, whole_spec((1, heads)), *part_specs(block_of)],
            out_specs=(
                whole_spec((tokens, 2 * heads)),
                whole_spec((tokens, 2 * heads)),
                whole_spec((group_chunks, 2 * STATE, CHUNK)),
                *part_specs(block_of),
            ),
            scratch_shapes=[
                pltpu.VMEM((tokens, 2 * heads), BF16),
                pltpu.VMEM((tokens, 2 * heads), BF16),
                pltpu.VMEM((blocks, STATE, channels), BF16),
                pltpu.VMEM((blocks, STATE, channels), BF16),
                pltpu.VMEM((blocks, 16, channels), F32),
                pltpu.VMEM((chunks, rows, CHUNK), BF16),
                pltpu.VMEM((chunks, rows, CHUNK), BF16),
                pltpu.VMEM((chunks, 2 * STATE, CHUNK), BF16),
                pltpu.VMEM((chunks, 2 * STATE, CHUNK), BF16),
                pltpu.VMEM((chunks, 2 * STATE, CHUNK), BF16),
                pltpu.SemaphoreType.DMA((chunks,)),
                pltpu.SemaphoreType.DMA((chunks,)),
                pltpu.SemaphoreType.DMA((chunks,)),
                pltpu.SemaphoreType.DMA((chunks,)),
            ],
            compiler_params=pltpu.CompilerParams(
                vmem_limit_bytes=VMEM_LIMIT, collective_id=0, has_side_effects=True
            ),
            name="exchange",
        )(
            doc_start,
            segment_order,
            seq_input,
            out_grad,
            own_write,
            own_read,
            step_size,
            rate_row,
            skip_row,
            seq_input,
            out_grad,
            own_write,
            own_read,
        )
    else:
        done = 0
        state_shape = jax.ShapeDtypeStruct((blocks, STATE, channels), BF16)
        message, pre, suf, e_cols, f_cols, whole_e, whole_f = pl.pallas_call(
            functools.partial(summary_kernel, blocks),
            grid=(chunks,),
            out_shape=(
                jax.ShapeDtypeStruct((chunks, rows, CHUNK), BF16),
                state_shape,
                state_shape,
                *[column_shape] * 4,
            ),
            in_specs=[smem, *chunk_specs(lambda i: i), *tables],
            out_specs=(
                pl.BlockSpec((1, rows, CHUNK), lambda i: (i, 0, 0)),
                pl.BlockSpec((blocks, STATE, CHUNK), lambda i: (0, 0, i)),
                pl.BlockSpec((blocks, STATE, CHUNK), lambda i: (0, 0, i)),
                *[whole_spec((tokens, 2 * heads))] * 4,
            ),
            scratch_shapes=[pltpu.VMEM((blocks, 16, CHUNK), F32)],
            compiler_params=params,
            name="summary",
        )(doc_start, seq_input, out_grad, own_write, own_read, step_size, rate_row)
        width = channels // seq_count
        message = jnp.transpose(message, (1, 0, 2)).reshape(rows, seq_count, width)
        message = jnp.transpose(message, (1, 0, 2))
        got = lax.all_to_all(message, "seq", split_axis=0, concat_axis=0, tiled=True)
        parts = pl.pallas_call(
            functools.partial(inner_kernel, blocks, span),
            grid=(groups, blocks),
            out_shape=part_shapes,
            in_specs=[
                smem,
                *part_specs(by_block),
                pl.BlockSpec((BLOCK, 2 * heads), lambda g, k: (k, 0)),
                pl.BlockSpec((BLOCK, 2 * heads), lambda g, k: (k, 0)),
                pl.BlockSpec((1, STATE, lanes), lambda g, k: (k, 0, g)),
                pl.BlockSpec((1, STATE, lanes), lambda g, k: (k, 0, g)),
                whole_spec((1, heads)),
            ],
            out_specs=part_specs(by_block),
            compiler_params=params,
            name="inner",
        )(doc_start, seq_input, out_grad, own_write, own_read, e_cols, f_cols, pre, suf, skip_row)
        order = jnp.zeros((seq_count,), jnp.int32).at[segment_order].set(
            jnp.arange(seq_count, dtype=jnp.int32)
        )
        answer = pl.pallas_call(
            functools.partial(chain_kernel, seq_count),
            out_shape=jax.ShapeDtypeStruct((seq_count, 2 * STATE, width), BF16),
            in_specs=[smem, pl.BlockSpec(memory_space=pltpu.VMEM)],
            out_specs=pl.BlockSpec(memory_space=pltpu.VMEM),
            compiler_params=params,
            name="chain",
        )(order, got)
        device = lax.all_to_all(answer, "seq", split_axis=0, concat_axis=0, tiled=True)
        device = jnp.transpose(device, (1, 0, 2)).reshape(2 * STATE, chunks, CHUNK)
        device = jnp.transpose(device, (1, 0, 2))

    def by_open_block(g, k):
        return (jnp.where(g < done, 0, k), jnp.maximum(g, done))

    def open_rows(g, k):
        return (jnp.where(g < done, 0, k), 0)

    mixed, input_grad, write_sum, read_sum = pl.pallas_call(
        functools.partial(finish_kernel, span, done),
        grid=(groups, blocks),
        out_shape=part_shapes,
        in_specs=[
            *part_specs(by_open_block),
            pl.BlockSpec((BLOCK, 2 * heads), open_rows),
            pl.BlockSpec((BLOCK, 2 * heads), open_rows),
            pl.BlockSpec((group_chunks, 2 * STATE, CHUNK), lambda g, k: (jnp.maximum(g - done, 0), 0, 0)),
            *part_specs(by_block),
        ],
        out_specs=part_specs(by_block),
        compiler_params=params,
        name="finish",
    )(seq_input, out_grad, own_write, own_read, whole_e, whole_f, device, *parts)

    for level in range(levels):
        other_write_sum, other_read_sum = partner(
            (write_sum.astype(BF16), read_sum.astype(BF16)), "head", level
        )
        write_sum = write_sum + other_write_sum.astype(F32)
        read_sum = read_sum + other_read_sum.astype(F32)
    own_width = groups * STATE // group_devices
    if group_devices > 1:
        own_first = head_rank % group_devices * own_width
        write_sum = lax.dynamic_slice_in_dim(write_sum, own_first, own_width, 1)
        read_sum = lax.dynamic_slice_in_dim(read_sum, own_first, own_width, 1)
    return mixed, input_grad, write_sum, read_sum


def solution(mesh):
    placed = (
        P("seq", "head"),
        P("head", "seq"),
        P("head"),
        P("head"),
        P("seq", "head"),
        P("seq", "head"),
        P("seq", "head"),
        P(),
        P(),
    )
    return jax.shard_map(
        on_device,
        mesh=mesh,
        in_specs=placed,
        out_specs=(P("seq", "head"), P("seq", "head"), P("seq", "head"), P("seq", "head")),
        check_vma=False,
    )
```

```python
import functools

import jax
import jax.numpy as jnp
from jax import lax
from jax.experimental import pallas as pl
from jax.experimental.pallas import tpu as pltpu
from jax.sharding import PartitionSpec as P

HEADS = 128
HEAD_DIM = 64
STATE = 128
GROUPS = 8
BLOCK = 256
CHUNK = 256
EXTRA = 16
VMEM_LIMIT = 34 * 1024 * 1024
FINISH_LIMIT = 16 * 1024 * 1024

F32 = jnp.float32
BF16 = jnp.bfloat16


def partner(block, axis, bit):
    count = lax.axis_size(axis)
    route = []
    for low in range(count):
        high = low | 1 << bit
        if high != low and high < count:
            route += [(low, high), (high, low)]
    return lax.ppermute(block, axis, route)


def dot_nn(a, b):
    return lax.dot_general(a, b, (((1,), (0,)), ((), ())), preferred_element_type=F32)


def dot_nt(a, b):
    return lax.dot_general(a, b, (((1,), (1,)), ((), ())), preferred_element_type=F32)


def dot_tn(a, b):
    return lax.dot_general(a, b, (((0,), (0,)), ((), ())), preferred_element_type=F32)


def iota(shape, dim):
    return lax.broadcasted_iota(jnp.int32, shape, dim)


def head_spread(heads, first_head, width):
    row = iota((heads, width), 0)
    return (row == first_head + iota((heads, width), 1) // HEAD_DIM).astype(F32).astype(BF16)


def head_spread_halves(heads, first_head, width):
    row = iota((2 * heads, width), 0)
    row = jnp.where(row >= heads, row - heads, row)
    return (row == first_head + iota((2 * heads, width), 1) // HEAD_DIM).astype(F32).astype(BF16)


def three_parts(value):
    high = value.astype(BF16)
    rest = value - high.astype(F32)
    mid = rest.astype(BF16)
    return high, mid, (rest - mid.astype(F32)).astype(BF16)


def spread_row(row, matrix):
    tall = jnp.broadcast_to(row, (8, row.shape[1]))
    return sum(dot_nn(part, matrix) for part in three_parts(tall))[0:1, :]


def token_setup(blocks, base, doc_ref, step_ref, rate_ref, e_ref, f_ref, whole_e_ref, whole_f_ref):
    heads = step_ref.shape[0]
    row, col = iota((heads, 2 * heads), 0), iota((heads, 2 * heads), 1)
    twice = ((row == col) | (row + heads == col)).astype(F32).astype(BF16)
    rate = spread_row(rate_ref[...], twice)
    row, col = iota((BLOCK, BLOCK), 0), iota((BLOCK, BLOCK), 1)
    lower = (row >= col).astype(F32).astype(BF16)
    eye = (row == col).astype(F32).astype(BF16)
    left = iota((BLOCK, 2 * heads), 1) < heads
    position = iota((BLOCK, 2 * heads), 0)

    def halves(value):
        top = value.astype(BF16).astype(F32)
        return jnp.where(left, top, value - top).astype(BF16)

    lead = jnp.ones((1, 2 * heads), F32)
    weights = []
    for k in range(blocks):
        rows = pl.ds(k * BLOCK, BLOCK)
        doc = doc_ref[base + k]
        step = step_ref[:, rows]
        parts = three_parts(jnp.concatenate([step, step], axis=0))
        cum = -rate * sum(dot_nt(lower, part) for part in parts)
        e = jnp.exp(cum)
        f = sum(dot_nt(eye, part) for part in parts) * jnp.exp(-cum)
        last = e[BLOCK - 1 : BLOCK, :]
        decay = jnp.where(doc == BLOCK, last, 0.0)
        e_ref[rows, :] = halves(e)
        f_ref[rows, :] = halves(f)
        whole_e_ref[rows, :] = halves(lead * jnp.where(position < doc, e, 0.0))
        lead = lead * decay
        weights.append((jnp.where(position >= doc, last * f, 0.0), decay))
    tail = jnp.ones((1, 2 * heads), F32)
    for k in reversed(range(blocks)):
        whole_f_ref[pl.ds(k * BLOCK, BLOCK), :] = halves(tail * weights[k][0])
        tail = tail * weights[k][1]


def summary(
    blocks, base, chunk, slot, lanes, doc_ref, x_ref, g_ref, b_ref, c_ref, e_ref, f_ref, msg_ref, pre_ref, suf_ref
):
    spread = head_spread_halves(e_ref.shape[1] // 2, chunk * (CHUNK // HEAD_DIM), CHUNK)
    position = iota((BLOCK, STATE), 0)
    ends, reads, decays, lasts = [], [], [], []
    for k in range(blocks):
        rows = pl.ds(k * BLOCK, BLOCK)
        doc = doc_ref[base + k]
        e_wide = dot_nn(e_ref[rows, :], spread)
        f_wide = dot_nn(f_ref[rows, :], spread)
        grad_in = (e_wide * g_ref[rows, :].astype(F32)).astype(BF16)
        data_in = (f_wide * x_ref[rows, :].astype(F32)).astype(BF16)
        write = jnp.where(position >= doc, b_ref[rows, :].astype(F32), 0.0).astype(BF16)
        read = jnp.where(position < doc, c_ref[rows, :].astype(F32), 0.0).astype(BF16)
        last = e_wide[BLOCK - 1 : BLOCK, :]
        ends.append(last * dot_tn(write, data_in))
        reads.append(dot_tn(read, grad_in))
        decays.append(jnp.where(doc == BLOCK, last, 0.0))
        lasts.append(last)
    state = jnp.zeros((STATE, CHUNK), F32)
    lead = jnp.ones((1, CHUNK), F32)
    for k in range(blocks):
        pre_ref[k, :, lanes] = state.astype(BF16)
        state = decays[k] * state + ends[k]
        lead = lead * decays[k]
    grad = jnp.zeros((STATE, CHUNK), F32)
    for k in reversed(range(blocks)):
        suf_ref[k, :, lanes] = (lasts[k] * grad).astype(BF16)
        grad = reads[k] + decays[k] * grad
    msg_ref[slot, :STATE, :] = state.astype(BF16)
    msg_ref[slot, STATE : 2 * STATE, :] = grad.astype(BF16)
    full = jnp.broadcast_to(lead, (EXTRA, CHUNK))
    top = full.astype(BF16).astype(F32)
    msg_ref[slot, 2 * STATE :, :] = jnp.where(iota((EXTRA, CHUNK), 0) == 0, top, full - top).astype(BF16)


def inner_block(
    doc, first_head, e, f, x_ref, g_ref, b_ref, c_ref, state, grad, skip_ref, y_ref, dx_ref, dw_ref, dr_ref
):
    heads = e.shape[1] // 2
    width = x_ref.shape[1]
    spread = head_spread_halves(heads, first_head, width)
    e_wide, f_wide = dot_nn(e, spread), dot_nn(f, spread)
    skip = spread_row(skip_ref[...], head_spread(heads, first_head, width))
    x, g = x_ref[...].astype(F32), g_ref[...].astype(F32)
    grad_in = (e_wide * g).astype(BF16)
    data_in = (f_wide * x).astype(BF16)
    position = iota((BLOCK, STATE), 0)
    b, c = b_ref[...], c_ref[...]
    write_on, read_on = position >= doc, position < doc
    write = jnp.where(write_on, b.astype(F32), 0.0).astype(BF16)
    read = jnp.where(read_on, c.astype(F32), 0.0).astype(BF16)
    row, col = iota((BLOCK, BLOCK), 0), iota((BLOCK, BLOCK), 1)
    keep = (row >= col) & ((row < doc) | (col >= doc))
    keep_t = (col >= row) & ((col < doc) | (row >= doc))
    score = jnp.where(keep, dot_nt(c, b), 0.0).astype(BF16)
    score_t = jnp.where(keep_t, dot_nt(b, c), 0.0).astype(BF16)
    y_ref[...] = (e_wide * (dot_nn(score, data_in) + dot_nn(read, state)) + skip * x).astype(BF16)
    dx_ref[...] = (f_wide * (dot_nn(score_t, grad_in) + dot_nn(write, grad)) + skip * g).astype(BF16)
    score_grad = jnp.where(keep, dot_nt(grad_in, data_in), 0.0).astype(BF16)
    dw_ref[...] = dot_tn(score_grad, c) + jnp.where(write_on, dot_nt(data_in, grad), 0.0)
    dr_ref[...] = dot_nn(score_grad, b) + jnp.where(read_on, dot_nt(grad_in, state), 0.0)


def summary_kernel(
    blocks, doc_ref, x_ref, g_ref, b_ref, c_ref, step_ref, rate_ref, msg_ref, pre_ref, suf_ref, e_ref, f_ref, we_ref, wf_ref
):
    chunk = pl.program_id(0)
    base = lax.axis_index("seq") * blocks

    @pl.when(chunk == 0)
    def _():
        token_setup(blocks, base, doc_ref, step_ref, rate_ref, e_ref, f_ref, we_ref, wf_ref)

    lanes = slice(None)
    summary(blocks, base, chunk, 0, lanes, doc_ref, x_ref, g_ref, b_ref, c_ref, e_ref, f_ref, msg_ref, pre_ref, suf_ref)


def inner_kernel(
    blocks, span, doc_ref, x_ref, g_ref, b_ref, c_ref, e_ref, f_ref, pre_ref, suf_ref, skip_ref, y_ref, dx_ref, dw_ref, dr_ref
):
    group, k = pl.program_id(0), pl.program_id(1)
    doc = doc_ref[lax.axis_index("seq") * blocks + k]
    inner_block(
        doc, group * span, e_ref[...], f_ref[...], x_ref, g_ref, b_ref, c_ref, pre_ref[0], suf_ref[0], skip_ref, y_ref, dx_ref, dw_ref, dr_ref
    )


def shard_at(place_ref, count, place):
    found = 0
    for shard in range(1, count):
        found = jnp.where(place_ref[shard] == place, shard, found)
    return found


def chain_kernel(count, order_ref, got_ref, out_ref):
    width = got_ref.shape[-1]

    def decay_of(shard):
        pair = got_ref[shard, 2 * STATE :, :].astype(F32)
        return pair[0:1, :] + pair[1:2, :]

    def forward(place, state):
        shard = order_ref[place]
        out_ref[shard, :STATE, :] = state.astype(BF16)
        return decay_of(shard) * state + got_ref[shard, :STATE, :].astype(F32)

    def backward(step, grad):
        shard = order_ref[count - 1 - step]
        out_ref[shard, STATE:, :] = grad.astype(BF16)
        return decay_of(shard) * grad + got_ref[shard, STATE : 2 * STATE, :].astype(F32)

    empty = jnp.zeros((STATE, width), F32)
    lax.fori_loop(0, count, forward, empty)
    lax.fori_loop(0, count, backward, empty)


def owner_at(step, count):
    return lax.rem(step, 2) * (count // 2) + step // 2


def exchange_kernel(
    blocks,
    span,
    groups,
    count,
    doc_ref,
    place_ref,
    x_ref,
    g_ref,
    b_ref,
    c_ref,
    step_ref,
    rate_ref,
    skip_ref,
    bx_ref,
    bg_ref,
    bb_ref,
    bc_ref,
    we_ref,
    wf_ref,
    dev_ref,
    y_ref,
    dx_ref,
    dw_ref,
    dr_ref,
    e_ref,
    f_ref,
    pre,
    suf,
    msg,
    got,
    chain,
    answer,
    back,
    send_sem,
    recv_sem,
    back_send_sem,
    back_recv_sem,
):
    step = pl.program_id(0)
    me = lax.axis_index("seq")
    base = me * blocks
    barrier = pltpu.get_barrier_semaphore()
    steps = count + groups * blocks

    def outward(owner, source):
        return pltpu.make_async_remote_copy(
            src_ref=msg.at[owner],
            dst_ref=got.at[source],
            send_sem=send_sem.at[owner],
            recv_sem=recv_sem.at[source],
            device_id={"seq": owner},
            device_id_type=pl.DeviceIdType.MESH,
        )

    def homeward(shard, source):
        return pltpu.make_async_remote_copy(
            src_ref=answer.at[shard],
            dst_ref=back.at[source],
            send_sem=back_send_sem.at[shard],
            recv_sem=back_recv_sem.at[source],
            device_id={"seq": shard},
            device_id_type=pl.DeviceIdType.MESH,
        )

    @pl.when(step == 0)
    def _():
        for ahead in range(1, count):
            pl.semaphore_signal(
                barrier,
                inc=1,
                device_id={"seq": lax.rem(me + ahead, count)},
                device_id_type=pl.DeviceIdType.MESH,
            )
        token_setup(blocks, base, doc_ref, step_ref, rate_ref, e_ref, f_ref, we_ref, wf_ref)

    @pl.when(step < count)
    def _():
        owner = owner_at(step, count)
        lanes = pl.ds(pl.multiple_of(owner * CHUNK, CHUNK), CHUNK)
        summary(
            blocks, base, owner, owner, lanes, doc_ref, x_ref, g_ref, b_ref, c_ref, e_ref, f_ref, msg, pre, suf
        )

        @pl.when(step == 0)
        def _():
            pl.semaphore_wait(barrier, count - 1)

        @pl.when(owner != me)
        def _():
            outward(owner, me).start()

        @pl.when(owner == me)
        def _():
            got[me] = msg[owner]

    @pl.when((step >= count) & (step < steps))
    def _():
        group = (step - count) // blocks
        k = lax.rem(step - count, blocks)
        rows = pl.ds(pl.multiple_of(k * BLOCK, BLOCK), BLOCK)
        wide = span * HEAD_DIM
        lanes = pl.ds(pl.multiple_of(group * wide, wide), wide)
        inner_block(
            doc_ref[base + k],
            group * span,
            e_ref[rows, :],
            f_ref[rows, :],
            bx_ref,
            bg_ref,
            bb_ref,
            bc_ref,
            pre[k, :, lanes],
            suf[k, :, lanes],
            skip_ref,
            y_ref,
            dx_ref,
            dw_ref,
            dr_ref,
        )

    half = count // 2
    turn = 2 * lax.rem(me, half) + me // half
    chain_step = count + (turn * (groups * blocks * 5 // 8)) // (count - 1)

    @pl.when(step == chain_step)
    def _():
        for shard in range(count):

            @pl.when(me != shard)
            def _():
                outward(shard, shard).wait_recv()

        def decay_of(shard):
            pair = got[shard, 2 * STATE :, :].astype(F32)
            return pair[0:1, :] + pair[1:2, :]

        order = [shard_at(place_ref, count, place) for place in range(count)]
        state = jnp.zeros((STATE, CHUNK), F32)
        for place in range(count):
            shard = order[place]
            chain[place, :STATE, :] = state.astype(BF16)
            state = decay_of(shard) * state + got[shard, :STATE, :].astype(F32)
        grad = jnp.zeros((STATE, CHUNK), F32)
        for place in reversed(range(count)):
            shard = order[place]
            chain[place, STATE:, :] = grad.astype(BF16)
            grad = decay_of(shard) * grad + got[shard, STATE : 2 * STATE, :].astype(F32)
        for shard in range(count):
            answer[shard] = chain[place_ref[shard]]

            @pl.when(me != shard)
            def _():
                homeward(shard, me).start()

        back[me] = answer[me]

    @pl.when(step == steps)
    def _():
        for shard in range(count):

            @pl.when(me != shard)
            def _():
                homeward(shard, shard).wait_recv()

        for shard in range(count):

            @pl.when(me != shard)
            def _():
                outward(shard, me).wait_send()
                homeward(shard, me).wait_send()

        dev_ref[...] = back[...]


def finish_kernel(
    span, x_ref, g_ref, b_ref, c_ref, e_ref, f_ref, dev_ref, yp_ref, dxp_ref, dwp_ref, drp_ref, y_ref, dx_ref, dw_ref, dr_ref
):
    spread = head_spread_halves(e_ref.shape[1] // 2, pl.program_id(0) * span, span * HEAD_DIM)
    e_wide = dot_nn(e_ref[...], spread)
    f_wide = dot_nn(f_ref[...], spread)
    grad_in = (e_wide * g_ref[...].astype(F32)).astype(BF16)
    data_in = (f_wide * x_ref[...].astype(F32)).astype(BF16)
    parts = range(dev_ref.shape[0])
    state = jnp.concatenate([dev_ref[j, :STATE, :] for j in parts], axis=1)
    grad = jnp.concatenate([dev_ref[j, STATE:, :] for j in parts], axis=1)
    y_ref[...] = (yp_ref[...].astype(F32) + e_wide * dot_nn(c_ref[...], state)).astype(BF16)
    dx_ref[...] = (dxp_ref[...].astype(F32) + f_wide * dot_nn(b_ref[...], grad)).astype(BF16)
    dw_ref[...] = dwp_ref[...] + dot_nt(data_in, grad)
    dr_ref[...] = drp_ref[...] + dot_nt(grad_in, state)


def on_device(
    seq_input,
    step_size,
    decay_rate,
    skip_gain,
    state_write,
    state_read,
    out_grad,
    segment_order,
    doc_start,
):
    heads = decay_rate.shape[0]
    group_heads = HEADS // GROUPS
    span = min(heads, group_heads)
    groups = heads // span
    group_devices = max(1, group_heads // heads)
    levels = group_devices.bit_length() - 1
    tokens = seq_input.shape[0]
    blocks = tokens // BLOCK
    channels = heads * HEAD_DIM
    chunks = channels // CHUNK
    group_chunks = chunks // groups
    seq_count = lax.axis_size("seq")
    head_rank = lax.axis_index("head")
    own_write, own_read = (state_write, state_read)
    for level in range(levels):
        other_write, other_read = partner((own_write, own_read), "head", level)
        upper_half = head_rank >> level & 1 == 1
        own_write = jnp.where(
            upper_half,
            jnp.concatenate([other_write, own_write], 1),
            jnp.concatenate([own_write, other_write], 1),
        )
        own_read = jnp.where(
            upper_half,
            jnp.concatenate([other_read, own_read], 1),
            jnp.concatenate([own_read, other_read], 1),
        )
    rate_row = decay_rate.reshape(1, heads)
    skip_row = skip_gain.reshape(1, heads)
    smem = pl.BlockSpec(memory_space=pltpu.SMEM)
    params = pltpu.CompilerParams(vmem_limit_bytes=VMEM_LIMIT)
    rows = 2 * STATE + EXTRA
    lanes = span * HEAD_DIM
    column_shape = jax.ShapeDtypeStruct((tokens, 2 * heads), BF16)
    part_shapes = (
        jax.ShapeDtypeStruct((tokens, channels), BF16),
        jax.ShapeDtypeStruct((tokens, channels), BF16),
        jax.ShapeDtypeStruct((tokens, groups * STATE), F32),
        jax.ShapeDtypeStruct((tokens, groups * STATE), F32),
    )

    def whole_spec(shape):
        return pl.BlockSpec(shape, lambda *place: (0,) * len(shape))

    def part_specs(where):
        return (
            pl.BlockSpec((BLOCK, lanes), where),
            pl.BlockSpec((BLOCK, lanes), where),
            pl.BlockSpec((BLOCK, STATE), where),
            pl.BlockSpec((BLOCK, STATE), where),
        )

    def chunk_specs(chunk_of):
        return [
            pl.BlockSpec((tokens, CHUNK), lambda i: (0, chunk_of(i))),
            pl.BlockSpec((tokens, CHUNK), lambda i: (0, chunk_of(i))),
            pl.BlockSpec((tokens, STATE), lambda i: (0, chunk_of(i) // group_chunks)),
            pl.BlockSpec((tokens, STATE), lambda i: (0, chunk_of(i) // group_chunks)),
        ]

    def by_block(g, k):
        return (k, g)

    tables = [whole_spec((heads, tokens)), whole_spec((1, heads))]
    if chunks == seq_count:

        def served(i):
            return owner_at(jnp.minimum(i, chunks - 1), chunks)

        def block_of(i):
            place = jnp.clip(i - chunks, 0, groups * blocks - 1)
            return (lax.rem(place, blocks), place // blocks)

        whole_e, whole_f, device, *parts = pl.pallas_call(
            functools.partial(exchange_kernel, blocks, span, groups, seq_count),
            grid=(chunks + groups * blocks + 1,),
            out_shape=(
                column_shape,
                column_shape,
                jax.ShapeDtypeStruct((chunks, 2 * STATE, CHUNK), BF16),
                *part_shapes,
            ),
            in_specs=[smem, smem, *chunk_specs(served), *tables, whole_spec((1, heads)), *part_specs(block_of)],
            out_specs=(
                whole_spec((tokens, 2 * heads)),
                whole_spec((tokens, 2 * heads)),
                whole_spec((chunks, 2 * STATE, CHUNK)),
                *part_specs(block_of),
            ),
            scratch_shapes=[
                pltpu.VMEM((tokens, 2 * heads), BF16),
                pltpu.VMEM((tokens, 2 * heads), BF16),
                pltpu.VMEM((blocks, STATE, channels), BF16),
                pltpu.VMEM((blocks, STATE, channels), BF16),
                pltpu.VMEM((chunks, rows, CHUNK), BF16),
                pltpu.VMEM((chunks, rows, CHUNK), BF16),
                pltpu.VMEM((chunks, 2 * STATE, CHUNK), BF16),
                pltpu.VMEM((chunks, 2 * STATE, CHUNK), BF16),
                pltpu.VMEM((chunks, 2 * STATE, CHUNK), BF16),
                pltpu.SemaphoreType.DMA((chunks,)),
                pltpu.SemaphoreType.DMA((chunks,)),
                pltpu.SemaphoreType.DMA((chunks,)),
                pltpu.SemaphoreType.DMA((chunks,)),
            ],
            compiler_params=pltpu.CompilerParams(
                vmem_limit_bytes=VMEM_LIMIT, collective_id=0, has_side_effects=True
            ),
            name="exchange",
        )(
            doc_start,
            segment_order,
            seq_input,
            out_grad,
            own_write,
            own_read,
            step_size,
            rate_row,
            skip_row,
            seq_input,
            out_grad,
            own_write,
            own_read,
        )
    else:
        state_shape = jax.ShapeDtypeStruct((blocks, STATE, channels), BF16)
        message, pre, suf, e_cols, f_cols, whole_e, whole_f = pl.pallas_call(
            functools.partial(summary_kernel, blocks),
            grid=(chunks,),
            out_shape=(
                jax.ShapeDtypeStruct((chunks, rows, CHUNK), BF16),
                state_shape,
                state_shape,
                *[column_shape] * 4,
            ),
            in_specs=[smem, *chunk_specs(lambda i: i), *tables],
            out_specs=(
                pl.BlockSpec((1, rows, CHUNK), lambda i: (i, 0, 0)),
                pl.BlockSpec((blocks, STATE, CHUNK), lambda i: (0, 0, i)),
                pl.BlockSpec((blocks, STATE, CHUNK), lambda i: (0, 0, i)),
                *[whole_spec((tokens, 2 * heads))] * 4,
            ),
            compiler_params=params,
            name="summary",
        )(doc_start, seq_input, out_grad, own_write, own_read, step_size, rate_row)
        width = channels // seq_count
        message = jnp.transpose(message, (1, 0, 2)).reshape(rows, seq_count, width)
        message = jnp.transpose(message, (1, 0, 2))
        got = lax.all_to_all(message, "seq", split_axis=0, concat_axis=0, tiled=True)
        parts = pl.pallas_call(
            functools.partial(inner_kernel, blocks, span),
            grid=(groups, blocks),
            out_shape=part_shapes,
            in_specs=[
                smem,
                *part_specs(by_block),
                pl.BlockSpec((BLOCK, 2 * heads), lambda g, k: (k, 0)),
                pl.BlockSpec((BLOCK, 2 * heads), lambda g, k: (k, 0)),
                pl.BlockSpec((1, STATE, lanes), lambda g, k: (k, 0, g)),
                pl.BlockSpec((1, STATE, lanes), lambda g, k: (k, 0, g)),
                whole_spec((1, heads)),
            ],
            out_specs=part_specs(by_block),
            compiler_params=params,
            name="inner",
        )(doc_start, seq_input, out_grad, own_write, own_read, e_cols, f_cols, pre, suf, skip_row)
        order = jnp.zeros((seq_count,), jnp.int32).at[segment_order].set(
            jnp.arange(seq_count, dtype=jnp.int32)
        )
        answer = pl.pallas_call(
            functools.partial(chain_kernel, seq_count),
            out_shape=jax.ShapeDtypeStruct((seq_count, 2 * STATE, width), BF16),
            in_specs=[smem, pl.BlockSpec(memory_space=pltpu.VMEM)],
            out_specs=pl.BlockSpec(memory_space=pltpu.VMEM),
            compiler_params=params,
            name="chain",
        )(order, got)
        device = lax.all_to_all(answer, "seq", split_axis=0, concat_axis=0, tiled=True)
        device = jnp.transpose(device, (1, 0, 2)).reshape(2 * STATE, chunks, CHUNK)
        device = jnp.transpose(device, (1, 0, 2))

    mixed, input_grad, write_sum, read_sum = pl.pallas_call(
        functools.partial(finish_kernel, span),
        grid=(groups, blocks),
        out_shape=part_shapes,
        in_specs=[
            *part_specs(by_block),
            pl.BlockSpec((BLOCK, 2 * heads), lambda g, k: (k, 0)),
            pl.BlockSpec((BLOCK, 2 * heads), lambda g, k: (k, 0)),
            pl.BlockSpec((group_chunks, 2 * STATE, CHUNK), lambda g, k: (g, 0, 0)),
            *part_specs(by_block),
        ],
        out_specs=part_specs(by_block),
        compiler_params=pltpu.CompilerParams(vmem_limit_bytes=FINISH_LIMIT),
        name="finish",
    )(seq_input, out_grad, own_write, own_read, whole_e, whole_f, device, *parts)

    for level in range(levels):
        other_write_sum, other_read_sum = partner(
            (write_sum.astype(BF16), read_sum.astype(BF16)), "head", level
        )
        write_sum = write_sum + other_write_sum.astype(F32)
        read_sum = read_sum + other_read_sum.astype(F32)
    own_width = groups * STATE // group_devices
    if group_devices > 1:
        own_first = head_rank % group_devices * own_width
        write_sum = lax.dynamic_slice_in_dim(write_sum, own_first, own_width, 1)
        read_sum = lax.dynamic_slice_in_dim(read_sum, own_first, own_width, 1)
    return mixed, input_grad, write_sum, read_sum


def solution(mesh):
    placed = (
        P("seq", "head"),
        P("head", "seq"),
        P("head"),
        P("head"),
        P("seq", "head"),
        P("seq", "head"),
        P("seq", "head"),
        P(),
        P(),
    )
    return jax.shard_map(
        on_device,
        mesh=mesh,
        in_specs=placed,
        out_specs=(P("seq", "head"), P("seq", "head"), P("seq", "head"), P("seq", "head")),
        check_vma=False,
    )
```

```python
import functools

import jax
import jax.numpy as jnp
from jax import lax
from jax.experimental import pallas as pl
from jax.experimental.pallas import tpu as pltpu
from jax.sharding import PartitionSpec as P

HEADS = 128
HEAD_DIM = 64
STATE = 128
GROUPS = 8
BLOCK = 256
CHUNK = 256
EXTRA = 16
VMEM_LIMIT = 60 * 1024 * 1024
FINISH_LIMIT = 60 * 1024 * 1024

F32 = jnp.float32
BF16 = jnp.bfloat16


def partner(block, axis, bit):
    count = lax.axis_size(axis)
    route = []
    for low in range(count):
        high = low | 1 << bit
        if high != low and high < count:
            route += [(low, high), (high, low)]
    return lax.ppermute(block, axis, route)


def dot_nn(a, b):
    return lax.dot_general(a, b, (((1,), (0,)), ((), ())), preferred_element_type=F32)


def dot_nt(a, b):
    return lax.dot_general(a, b, (((1,), (1,)), ((), ())), preferred_element_type=F32)


def dot_tn(a, b):
    return lax.dot_general(a, b, (((0,), (0,)), ((), ())), preferred_element_type=F32)


def iota(shape, dim):
    return lax.broadcasted_iota(jnp.int32, shape, dim)


def head_spread(heads, first_head, width):
    row = iota((heads, width), 0)
    return (row == first_head + iota((heads, width), 1) // HEAD_DIM).astype(F32).astype(BF16)


def head_spread_halves(heads, first_head, width):
    row = iota((2 * heads, width), 0)
    row = jnp.where(row >= heads, row - heads, row)
    return (row == first_head + iota((2 * heads, width), 1) // HEAD_DIM).astype(F32).astype(BF16)


def three_parts(value):
    high = value.astype(BF16)
    rest = value - high.astype(F32)
    mid = rest.astype(BF16)
    return high, mid, (rest - mid.astype(F32)).astype(BF16)


def spread_row(row, matrix):
    tall = jnp.broadcast_to(row, (8, row.shape[1]))
    return sum(dot_nn(part, matrix) for part in three_parts(tall))[0:1, :]


def token_setup(blocks, base, doc_ref, step_ref, rate_ref, e_ref, f_ref, whole_e_ref, whole_f_ref):
    heads = step_ref.shape[0]
    row, col = iota((heads, 2 * heads), 0), iota((heads, 2 * heads), 1)
    twice = ((row == col) | (row + heads == col)).astype(F32).astype(BF16)
    rate = spread_row(rate_ref[...], twice)
    row, col = iota((BLOCK, BLOCK), 0), iota((BLOCK, BLOCK), 1)
    lower = (row >= col).astype(F32).astype(BF16)
    eye = (row == col).astype(F32).astype(BF16)
    left = iota((BLOCK, 2 * heads), 1) < heads
    position = iota((BLOCK, 2 * heads), 0)

    def halves(value):
        top = value.astype(BF16).astype(F32)
        return jnp.where(left, top, value - top).astype(BF16)

    lead = jnp.ones((1, 2 * heads), F32)
    weights = []
    for k in range(blocks):
        rows = pl.ds(k * BLOCK, BLOCK)
        doc = doc_ref[base + k]
        step = step_ref[:, rows]
        parts = three_parts(jnp.concatenate([step, step], axis=0))
        cum = -rate * sum(dot_nt(lower, part) for part in parts)
        e = jnp.exp(cum)
        f = sum(dot_nt(eye, part) for part in parts) * jnp.exp(-cum)
        last = e[BLOCK - 1 : BLOCK, :]
        decay = jnp.where(doc == BLOCK, last, 0.0)
        e_ref[rows, :] = halves(e)
        f_ref[rows, :] = halves(f)
        whole_e_ref[rows, :] = halves(lead * jnp.where(position < doc, e, 0.0))
        lead = lead * decay
        weights.append((jnp.where(position >= doc, last * f, 0.0), decay))
    tail = jnp.ones((1, 2 * heads), F32)
    for k in reversed(range(blocks)):
        whole_f_ref[pl.ds(k * BLOCK, BLOCK), :] = halves(tail * weights[k][0])
        tail = tail * weights[k][1]


def summary(
    blocks, base, chunk, slot, lanes, doc_ref, x_ref, g_ref, b_ref, c_ref, e_ref, f_ref, msg_ref, pre_ref, suf_ref
):
    spread = head_spread_halves(e_ref.shape[1] // 2, chunk * (CHUNK // HEAD_DIM), CHUNK)
    position = iota((BLOCK, STATE), 0)
    ends, reads, decays, lasts = [], [], [], []
    for k in range(blocks):
        rows = pl.ds(k * BLOCK, BLOCK)
        doc = doc_ref[base + k]
        e_wide = dot_nn(e_ref[rows, :], spread)
        f_wide = dot_nn(f_ref[rows, :], spread)
        grad_in = (e_wide * g_ref[rows, :].astype(F32)).astype(BF16)
        data_in = (f_wide * x_ref[rows, :].astype(F32)).astype(BF16)
        write = jnp.where(position >= doc, b_ref[rows, :].astype(F32), 0.0).astype(BF16)
        read = jnp.where(position < doc, c_ref[rows, :].astype(F32), 0.0).astype(BF16)
        last = e_wide[BLOCK - 1 : BLOCK, :]
        ends.append(last * dot_tn(write, data_in))
        reads.append(dot_tn(read, grad_in))
        decays.append(jnp.where(doc == BLOCK, last, 0.0))
        lasts.append(last)
    state = jnp.zeros((STATE, CHUNK), F32)
    lead = jnp.ones((1, CHUNK), F32)
    for k in range(blocks):
        pre_ref[k, :, lanes] = state.astype(BF16)
        state = decays[k] * state + ends[k]
        lead = lead * decays[k]
    grad = jnp.zeros((STATE, CHUNK), F32)
    for k in reversed(range(blocks)):
        suf_ref[k, :, lanes] = (lasts[k] * grad).astype(BF16)
        grad = reads[k] + decays[k] * grad
    msg_ref[slot, :STATE, :] = state.astype(BF16)
    msg_ref[slot, STATE : 2 * STATE, :] = grad.astype(BF16)
    full = jnp.broadcast_to(lead, (EXTRA, CHUNK))
    top = full.astype(BF16).astype(F32)
    msg_ref[slot, 2 * STATE :, :] = jnp.where(iota((EXTRA, CHUNK), 0) == 0, top, full - top).astype(BF16)


def inner_block(
    doc, first_head, e, f, x_ref, g_ref, b_ref, c_ref, state, grad, skip_ref, y_ref, dx_ref, dw_ref, dr_ref
):
    heads = e.shape[1] // 2
    width = x_ref.shape[1]
    spread = head_spread_halves(heads, first_head, width)
    e_wide, f_wide = dot_nn(e, spread), dot_nn(f, spread)
    skip = spread_row(skip_ref[...], head_spread(heads, first_head, width))
    x, g = x_ref[...].astype(F32), g_ref[...].astype(F32)
    grad_in = (e_wide * g).astype(BF16)
    data_in = (f_wide * x).astype(BF16)
    position = iota((BLOCK, STATE), 0)
    b, c = b_ref[...], c_ref[...]
    write_on, read_on = position >= doc, position < doc
    write = jnp.where(write_on, b.astype(F32), 0.0).astype(BF16)
    read = jnp.where(read_on, c.astype(F32), 0.0).astype(BF16)
    row, col = iota((BLOCK, BLOCK), 0), iota((BLOCK, BLOCK), 1)
    keep = (row >= col) & ((row < doc) | (col >= doc))
    keep_t = (col >= row) & ((col < doc) | (row >= doc))
    score = jnp.where(keep, dot_nt(c, b), 0.0).astype(BF16)
    score_t = jnp.where(keep_t, dot_nt(b, c), 0.0).astype(BF16)
    y_ref[...] = (e_wide * (dot_nn(score, data_in) + dot_nn(read, state)) + skip * x).astype(BF16)
    dx_ref[...] = (f_wide * (dot_nn(score_t, grad_in) + dot_nn(write, grad)) + skip * g).astype(BF16)
    score_grad = jnp.where(keep, dot_nt(grad_in, data_in), 0.0).astype(BF16)
    dw_ref[...] = dot_tn(score_grad, c) + jnp.where(write_on, dot_nt(data_in, grad), 0.0)
    dr_ref[...] = dot_nn(score_grad, b) + jnp.where(read_on, dot_nt(grad_in, state), 0.0)


def summary_kernel(
    blocks, doc_ref, x_ref, g_ref, b_ref, c_ref, step_ref, rate_ref, msg_ref, pre_ref, suf_ref, e_ref, f_ref, we_ref, wf_ref
):
    chunk = pl.program_id(0)
    base = lax.axis_index("seq") * blocks

    @pl.when(chunk == 0)
    def _():
        token_setup(blocks, base, doc_ref, step_ref, rate_ref, e_ref, f_ref, we_ref, wf_ref)

    lanes = slice(None)
    summary(blocks, base, chunk, 0, lanes, doc_ref, x_ref, g_ref, b_ref, c_ref, e_ref, f_ref, msg_ref, pre_ref, suf_ref)


def inner_kernel(
    blocks, span, doc_ref, x_ref, g_ref, b_ref, c_ref, e_ref, f_ref, pre_ref, suf_ref, skip_ref, y_ref, dx_ref, dw_ref, dr_ref
):
    group, k = pl.program_id(0), pl.program_id(1)
    doc = doc_ref[lax.axis_index("seq") * blocks + k]
    inner_block(
        doc, group * span, e_ref[...], f_ref[...], x_ref, g_ref, b_ref, c_ref, pre_ref[0], suf_ref[0], skip_ref, y_ref, dx_ref, dw_ref, dr_ref
    )


def shard_at(place_ref, count, place):
    found = 0
    for shard in range(1, count):
        found = jnp.where(place_ref[shard] == place, shard, found)
    return found


def chain_kernel(count, order_ref, got_ref, out_ref):
    width = got_ref.shape[-1]

    def decay_of(shard):
        pair = got_ref[shard, 2 * STATE :, :].astype(F32)
        return pair[0:1, :] + pair[1:2, :]

    def forward(place, state):
        shard = order_ref[place]
        out_ref[shard, :STATE, :] = state.astype(BF16)
        return decay_of(shard) * state + got_ref[shard, :STATE, :].astype(F32)

    def backward(step, grad):
        shard = order_ref[count - 1 - step]
        out_ref[shard, STATE:, :] = grad.astype(BF16)
        return decay_of(shard) * grad + got_ref[shard, STATE : 2 * STATE, :].astype(F32)

    empty = jnp.zeros((STATE, width), F32)
    lax.fori_loop(0, count, forward, empty)
    lax.fori_loop(0, count, backward, empty)


def owner_at(step, count):
    return lax.rem(step, 2) * (count // 2) + step // 2


def exchange_kernel(
    blocks,
    span,
    groups,
    count,
    doc_ref,
    place_ref,
    x_ref,
    g_ref,
    b_ref,
    c_ref,
    step_ref,
    rate_ref,
    skip_ref,
    bx_ref,
    bg_ref,
    bb_ref,
    bc_ref,
    we_ref,
    wf_ref,
    dev_ref,
    y_ref,
    dx_ref,
    dw_ref,
    dr_ref,
    e_ref,
    f_ref,
    pre,
    suf,
    msg,
    got,
    chain,
    answer,
    back,
    send_sem,
    recv_sem,
    back_send_sem,
    back_recv_sem,
):
    step = pl.program_id(0)
    me = lax.axis_index("seq")
    base = me * blocks
    barrier = pltpu.get_barrier_semaphore()
    steps = count + groups * blocks

    def outward(owner, source):
        return pltpu.make_async_remote_copy(
            src_ref=msg.at[owner],
            dst_ref=got.at[source],
            send_sem=send_sem.at[owner],
            recv_sem=recv_sem.at[source],
            device_id={"seq": owner},
            device_id_type=pl.DeviceIdType.MESH,
        )

    def homeward(shard, source):
        return pltpu.make_async_remote_copy(
            src_ref=answer.at[shard],
            dst_ref=back.at[source],
            send_sem=back_send_sem.at[shard],
            recv_sem=back_recv_sem.at[source],
            device_id={"seq": shard},
            device_id_type=pl.DeviceIdType.MESH,
        )

    @pl.when(step == 0)
    def _():
        for ahead in range(1, count):
            pl.semaphore_signal(
                barrier,
                inc=1,
                device_id={"seq": lax.rem(me + ahead, count)},
                device_id_type=pl.DeviceIdType.MESH,
            )
        token_setup(blocks, base, doc_ref, step_ref, rate_ref, e_ref, f_ref, we_ref, wf_ref)

    @pl.when(step < count)
    def _():
        owner = owner_at(step, count)
        lanes = pl.ds(pl.multiple_of(owner * CHUNK, CHUNK), CHUNK)
        summary(
            blocks, base, owner, owner, lanes, doc_ref, x_ref, g_ref, b_ref, c_ref, e_ref, f_ref, msg, pre, suf
        )

        @pl.when(step == 0)
        def _():
            pl.semaphore_wait(barrier, count - 1)

        @pl.when(owner != me)
        def _():
            outward(owner, me).start()

        @pl.when(owner == me)
        def _():
            got[me] = msg[owner]

    @pl.when((step >= count) & (step < steps))
    def _():
        group = (step - count) // blocks
        k = lax.rem(step - count, blocks)
        rows = pl.ds(pl.multiple_of(k * BLOCK, BLOCK), BLOCK)
        wide = span * HEAD_DIM
        lanes = pl.ds(pl.multiple_of(group * wide, wide), wide)
        inner_block(
            doc_ref[base + k],
            group * span,
            e_ref[rows, :],
            f_ref[rows, :],
            bx_ref,
            bg_ref,
            bb_ref,
            bc_ref,
            pre[k, :, lanes],
            suf[k, :, lanes],
            skip_ref,
            y_ref,
            dx_ref,
            dw_ref,
            dr_ref,
        )

    half = count // 2
    turn = 2 * lax.rem(me, half) + me // half
    chain_step = count + (turn * (groups * blocks * 5 // 8)) // (count - 1)

    @pl.when(step == chain_step)
    def _():
        for shard in range(count):

            @pl.when(me != shard)
            def _():
                outward(shard, shard).wait_recv()

        def decay_of(shard):
            pair = got[shard, 2 * STATE :, :].astype(F32)
            return pair[0:1, :] + pair[1:2, :]

        order = [shard_at(place_ref, count, place) for place in range(count)]
        state = jnp.zeros((STATE, CHUNK), F32)
        for place in range(count):
            shard = order[place]
            chain[place, :STATE, :] = state.astype(BF16)
            state = decay_of(shard) * state + got[shard, :STATE, :].astype(F32)
        grad = jnp.zeros((STATE, CHUNK), F32)
        for place in reversed(range(count)):
            shard = order[place]
            chain[place, STATE:, :] = grad.astype(BF16)
            grad = decay_of(shard) * grad + got[shard, STATE : 2 * STATE, :].astype(F32)
        for shard in range(count):
            answer[shard] = chain[place_ref[shard]]

            @pl.when(me != shard)
            def _():
                homeward(shard, me).start()

        back[me] = answer[me]

    @pl.when(step == steps)
    def _():
        for shard in range(count):

            @pl.when(me != shard)
            def _():
                homeward(shard, shard).wait_recv()

        for shard in range(count):

            @pl.when(me != shard)
            def _():
                outward(shard, me).wait_send()
                homeward(shard, me).wait_send()

        dev_ref[...] = back[...]


def finish_kernel(
    span, x_ref, g_ref, b_ref, c_ref, e_ref, f_ref, dev_ref, yp_ref, dxp_ref, dwp_ref, drp_ref, y_ref, dx_ref, dw_ref, dr_ref
):
    spread = head_spread_halves(e_ref.shape[1] // 2, pl.program_id(0) * span, span * HEAD_DIM)
    e_wide = dot_nn(e_ref[...], spread)
    f_wide = dot_nn(f_ref[...], spread)
    grad_in = (e_wide * g_ref[...].astype(F32)).astype(BF16)
    data_in = (f_wide * x_ref[...].astype(F32)).astype(BF16)
    parts = range(dev_ref.shape[0])
    state = jnp.concatenate([dev_ref[j, :STATE, :] for j in parts], axis=1)
    grad = jnp.concatenate([dev_ref[j, STATE:, :] for j in parts], axis=1)
    y_ref[...] = (yp_ref[...].astype(F32) + e_wide * dot_nn(c_ref[...], state)).astype(BF16)
    dx_ref[...] = (dxp_ref[...].astype(F32) + f_wide * dot_nn(b_ref[...], grad)).astype(BF16)
    dw_ref[...] = dwp_ref[...] + dot_nt(data_in, grad)
    dr_ref[...] = drp_ref[...] + dot_nt(grad_in, state)


def on_device(
    seq_input,
    step_size,
    decay_rate,
    skip_gain,
    state_write,
    state_read,
    out_grad,
    segment_order,
    doc_start,
):
    heads = decay_rate.shape[0]
    group_heads = HEADS // GROUPS
    span = min(heads, group_heads)
    groups = heads // span
    group_devices = max(1, group_heads // heads)
    levels = group_devices.bit_length() - 1
    tokens = seq_input.shape[0]
    blocks = tokens // BLOCK
    channels = heads * HEAD_DIM
    chunks = channels // CHUNK
    group_chunks = chunks // groups
    seq_count = lax.axis_size("seq")
    head_rank = lax.axis_index("head")
    own_write, own_read = (state_write, state_read)
    for level in range(levels):
        other_write, other_read = partner((own_write, own_read), "head", level)
        upper_half = head_rank >> level & 1 == 1
        own_write = jnp.where(
            upper_half,
            jnp.concatenate([other_write, own_write], 1),
            jnp.concatenate([own_write, other_write], 1),
        )
        own_read = jnp.where(
            upper_half,
            jnp.concatenate([other_read, own_read], 1),
            jnp.concatenate([own_read, other_read], 1),
        )
    rate_row = decay_rate.reshape(1, heads)
    skip_row = skip_gain.reshape(1, heads)
    smem = pl.BlockSpec(memory_space=pltpu.SMEM)
    params = pltpu.CompilerParams(vmem_limit_bytes=VMEM_LIMIT)
    rows = 2 * STATE + EXTRA
    lanes = span * HEAD_DIM
    column_shape = jax.ShapeDtypeStruct((tokens, 2 * heads), BF16)
    part_shapes = (
        jax.ShapeDtypeStruct((tokens, channels), BF16),
        jax.ShapeDtypeStruct((tokens, channels), BF16),
        jax.ShapeDtypeStruct((tokens, groups * STATE), F32),
        jax.ShapeDtypeStruct((tokens, groups * STATE), F32),
    )

    def whole_spec(shape):
        return pl.BlockSpec(shape, lambda *place: (0,) * len(shape))

    def part_specs(where):
        return (
            pl.BlockSpec((BLOCK, lanes), where),
            pl.BlockSpec((BLOCK, lanes), where),
            pl.BlockSpec((BLOCK, STATE), where),
            pl.BlockSpec((BLOCK, STATE), where),
        )

    def chunk_specs(chunk_of):
        return [
            pl.BlockSpec((tokens, CHUNK), lambda i: (0, chunk_of(i))),
            pl.BlockSpec((tokens, CHUNK), lambda i: (0, chunk_of(i))),
            pl.BlockSpec((tokens, STATE), lambda i: (0, chunk_of(i) // group_chunks)),
            pl.BlockSpec((tokens, STATE), lambda i: (0, chunk_of(i) // group_chunks)),
        ]

    def by_block(g, k):
        return (k, g)

    tables = [whole_spec((heads, tokens)), whole_spec((1, heads))]
    if chunks == seq_count:

        def served(i):
            return owner_at(jnp.minimum(i, chunks - 1), chunks)

        def block_of(i):
            place = jnp.clip(i - chunks, 0, groups * blocks - 1)
            return (lax.rem(place, blocks), place // blocks)

        whole_e, whole_f, device, *parts = pl.pallas_call(
            functools.partial(exchange_kernel, blocks, span, groups, seq_count),
            grid=(chunks + groups * blocks + 1,),
            out_shape=(
                column_shape,
                column_shape,
                jax.ShapeDtypeStruct((chunks, 2 * STATE, CHUNK), BF16),
                *part_shapes,
            ),
            in_specs=[smem, smem, *chunk_specs(served), *tables, whole_spec((1, heads)), *part_specs(block_of)],
            out_specs=(
                whole_spec((tokens, 2 * heads)),
                whole_spec((tokens, 2 * heads)),
                whole_spec((chunks, 2 * STATE, CHUNK)),
                *part_specs(block_of),
            ),
            scratch_shapes=[
                pltpu.VMEM((tokens, 2 * heads), BF16),
                pltpu.VMEM((tokens, 2 * heads), BF16),
                pltpu.VMEM((blocks, STATE, channels), BF16),
                pltpu.VMEM((blocks, STATE, channels), BF16),
                pltpu.VMEM((chunks, rows, CHUNK), BF16),
                pltpu.VMEM((chunks, rows, CHUNK), BF16),
                pltpu.VMEM((chunks, 2 * STATE, CHUNK), BF16),
                pltpu.VMEM((chunks, 2 * STATE, CHUNK), BF16),
                pltpu.VMEM((chunks, 2 * STATE, CHUNK), BF16),
                pltpu.SemaphoreType.DMA((chunks,)),
                pltpu.SemaphoreType.DMA((chunks,)),
                pltpu.SemaphoreType.DMA((chunks,)),
                pltpu.SemaphoreType.DMA((chunks,)),
            ],
            compiler_params=pltpu.CompilerParams(
                vmem_limit_bytes=VMEM_LIMIT, collective_id=0, has_side_effects=True
            ),
            name="exchange",
        )(
            doc_start,
            segment_order,
            seq_input,
            out_grad,
            own_write,
            own_read,
            step_size,
            rate_row,
            skip_row,
            seq_input,
            out_grad,
            own_write,
            own_read,
        )
    else:
        state_shape = jax.ShapeDtypeStruct((blocks, STATE, channels), BF16)
        message, pre, suf, e_cols, f_cols, whole_e, whole_f = pl.pallas_call(
            functools.partial(summary_kernel, blocks),
            grid=(chunks,),
            out_shape=(
                jax.ShapeDtypeStruct((chunks, rows, CHUNK), BF16),
                state_shape,
                state_shape,
                *[column_shape] * 4,
            ),
            in_specs=[smem, *chunk_specs(lambda i: i), *tables],
            out_specs=(
                pl.BlockSpec((1, rows, CHUNK), lambda i: (i, 0, 0)),
                pl.BlockSpec((blocks, STATE, CHUNK), lambda i: (0, 0, i)),
                pl.BlockSpec((blocks, STATE, CHUNK), lambda i: (0, 0, i)),
                *[whole_spec((tokens, 2 * heads))] * 4,
            ),
            compiler_params=params,
            name="summary",
        )(doc_start, seq_input, out_grad, own_write, own_read, step_size, rate_row)
        width = channels // seq_count
        message = jnp.transpose(message, (1, 0, 2)).reshape(rows, seq_count, width)
        message = jnp.transpose(message, (1, 0, 2))
        got = lax.all_to_all(message, "seq", split_axis=0, concat_axis=0, tiled=True)
        parts = pl.pallas_call(
            functools.partial(inner_kernel, blocks, span),
            grid=(groups, blocks),
            out_shape=part_shapes,
            in_specs=[
                smem,
                *part_specs(by_block),
                pl.BlockSpec((BLOCK, 2 * heads), lambda g, k: (k, 0)),
                pl.BlockSpec((BLOCK, 2 * heads), lambda g, k: (k, 0)),
                pl.BlockSpec((1, STATE, lanes), lambda g, k: (k, 0, g)),
                pl.BlockSpec((1, STATE, lanes), lambda g, k: (k, 0, g)),
                whole_spec((1, heads)),
            ],
            out_specs=part_specs(by_block),
            compiler_params=params,
            name="inner",
        )(doc_start, seq_input, out_grad, own_write, own_read, e_cols, f_cols, pre, suf, skip_row)
        order = jnp.zeros((seq_count,), jnp.int32).at[segment_order].set(
            jnp.arange(seq_count, dtype=jnp.int32)
        )
        answer = pl.pallas_call(
            functools.partial(chain_kernel, seq_count),
            out_shape=jax.ShapeDtypeStruct((seq_count, 2 * STATE, width), BF16),
            in_specs=[smem, pl.BlockSpec(memory_space=pltpu.VMEM)],
            out_specs=pl.BlockSpec(memory_space=pltpu.VMEM),
            compiler_params=params,
            name="chain",
        )(order, got)
        device = lax.all_to_all(answer, "seq", split_axis=0, concat_axis=0, tiled=True)
        device = jnp.transpose(device, (1, 0, 2)).reshape(2 * STATE, chunks, CHUNK)
        device = jnp.transpose(device, (1, 0, 2))

    mixed, input_grad, write_sum, read_sum = pl.pallas_call(
        functools.partial(finish_kernel, span),
        grid=(groups, blocks),
        out_shape=part_shapes,
        in_specs=[
            *part_specs(by_block),
            pl.BlockSpec((BLOCK, 2 * heads), lambda g, k: (k, 0)),
            pl.BlockSpec((BLOCK, 2 * heads), lambda g, k: (k, 0)),
            pl.BlockSpec((group_chunks, 2 * STATE, CHUNK), lambda g, k: (g, 0, 0)),
            *part_specs(by_block),
        ],
        out_specs=part_specs(by_block),
        compiler_params=pltpu.CompilerParams(vmem_limit_bytes=FINISH_LIMIT),
        name="finish",
    )(seq_input, out_grad, own_write, own_read, whole_e, whole_f, device, *parts)

    for level in range(levels):
        other_write_sum, other_read_sum = partner(
            (write_sum.astype(BF16), read_sum.astype(BF16)), "head", level
        )
        write_sum = write_sum + other_write_sum.astype(F32)
        read_sum = read_sum + other_read_sum.astype(F32)
    own_width = groups * STATE // group_devices
    if group_devices > 1:
        own_first = head_rank % group_devices * own_width
        write_sum = lax.dynamic_slice_in_dim(write_sum, own_first, own_width, 1)
        read_sum = lax.dynamic_slice_in_dim(read_sum, own_first, own_width, 1)
    return mixed, input_grad, write_sum, read_sum


def solution(mesh):
    placed = (
        P("seq", "head"),
        P("head", "seq"),
        P("head"),
        P("head"),
        P("seq", "head"),
        P("seq", "head"),
        P("seq", "head"),
        P(),
        P(),
    )
    return jax.shard_map(
        on_device,
        mesh=mesh,
        in_specs=placed,
        out_specs=(P("seq", "head"), P("seq", "head"), P("seq", "head"), P("seq", "head")),
        check_vma=False,
    )
```
